512 devices in a mesh: fsdp: 32 (over x_lo, z), side: 16 (over y, x_hi, core).
Axes of the slice: x: 4 (x_hi: 2, x_lo: 2; x = x_hi * 2 + x_lo), y: 4, z: 16, core: 2. Of those that a mesh axis runs over, the one named last changes fastest.
Arguments:
- attn_inputs: bfloat16 [65536, 5120], P(('side', 'fsdp')), may hold values from -24 to 24
- queries: bfloat16 [65536, 2560], P(('side', 'fsdp')), may hold values from -310 to 310
- key_vectors: bfloat16 [65536, 512], P(('side', 'fsdp')), may hold values from -12 to 12
- logp_grad: bfloat16 [65536, 2560], P(('side', 'fsdp')), may hold values from -24 to 24
- new_logp: float32 [65536], P(('side', 'fsdp')), may hold values from -6.5 to -0.01
- old_logp: float32 [65536], P(('side', 'fsdp')), may hold values from -4 to -0.05
- rewards: float32 [32], replicated, may hold values from -8 to 8
- group_ids: int32 [32], replicated, may hold values from 0 to 7
- lengths: int32 [32], replicated, may hold values from 1024 to 2048
- value_proj: bfloat16 [5120, 512], P('fsdp'), may hold values from -0.078125 to 0.078125
- first_moment: bfloat16 [5120, 512], P(('fsdp', 'side')), may hold values from -120 to 120
- second_moment: bfloat16 [5120, 512], P(('fsdp', 'side')), may hold values from 100 to 9984
Outputs:
- input_grad: bfloat16 [65536, 5120], P(('side', 'fsdp'))
- new_proj: bfloat16 [5120, 512], P('fsdp')
- new_first: bfloat16 [5120, 512], P(('fsdp', 'side'))
- new_second: bfloat16 [5120, 512], P(('fsdp', 'side'))
The draws below stay inside these ranges and needn't reach their ends.
All inputs are finite; a program needn't handle non-finite values.
Results may differ from the reference program's by a relative error of at most 0.03.
Values may be sent and summed in bfloat16 or wider, within the bound.
A program may use at most 64 MiB of HBM per device.

```python
import math
import jax
import jax.numpy as jnp
from jax import lax

D = 5120
QH = 20
KVH = 4
HEAD = 128
ROLLS = 2
TOK_DEV = 128
LENGTH = 2048
TOKENS = 4096
ALLROLL = 32
ALLTOK = 65536
GROUPS = 8
N_FSDP = 32
N_SIDE = 16


def attention_pair(key):
    base = jax.random.fold_in(key, 11)
    key_one, key_two = jax.random.split(base, 2)
    keys_drawn = jnp.clip(jax.random.normal(key_one, (ALLTOK, KVH * HEAD), jnp.float32), -6.0, 6.0)
    query_drawn = jnp.clip(jax.random.normal(key_two, (ALLTOK, QH * HEAD), jnp.float32), -6.0, 6.0)
    return (query_drawn, keys_drawn)


def log_probs(key):
    base = jax.random.fold_in(key, 23)
    key_one, key_two = jax.random.split(base, 2)
    old_value = jax.random.uniform(key_one, (ALLTOK,), jnp.float32, -4.0, -0.05)
    noise = jnp.clip(jax.random.normal(key_two, (ALLTOK,), jnp.float32), -4.0, 4.0)
    new_value = jnp.minimum(old_value + 0.3 * noise, -0.01)
    return (new_value, old_value)


def draw_queries(key, part):
    return attention_pair(key)[0].astype(jnp.bfloat16)


def draw_key_vectors(key, part):
    return attention_pair(key)[1].astype(jnp.bfloat16)


def draw_new_logp(key, part):
    return log_probs(key)[0]


def draw_old_logp(key, part):
    return log_probs(key)[1]


def with_ends(values, rng, low, largest):
    longest = values.shape.index(max(values.shape))
    spots = []
    for shift in (0, 1):
        where = [jax.random.randint(jax.random.fold_in(rng, axis), (), 0, length) for axis, length in enumerate(values.shape)]
        where[longest] = (where[longest] + shift) % values.shape[longest]
        spots.append(tuple(where))
    return values.at[spots[0]].set(low).at[spots[1]].set(largest)


def strengthened(entries, stream_key, source, target, blocks, factor):
    def block_of(dim):
        return (jnp.arange(entries.shape[dim]) // (entries.shape[dim] // blocks)).reshape((-1,) + (1,) * (entries.ndim - 1 - dim))

    one_side = jax.random.permutation(stream_key, blocks)[block_of(target)]
    far = (block_of(target) + blocks // 2) % blocks
    return jnp.where((block_of(source) == one_side) | (block_of(source) == far), factor * entries, entries)


def block_scale(own_key, shape, shards, low, high):
    gain, own = 1.0, jax.random.fold_in(own_key, 6)
    for dim, shards_of in shards:
        steps = jnp.exp(jax.random.uniform(jax.random.fold_in(own, dim), (shards_of,), jnp.float32, low / len(shards), high / len(shards)))
        gain = gain * jnp.repeat(steps, shape[dim] // shards_of).reshape([-1 if axis == dim else 1 for axis in range(len(shape))])
    return gain


def bell_draw(own_key, extent, deviation, bound, cuts=(), kind=jnp.bfloat16):
    values = deviation * jax.random.normal(own_key, extent, jnp.float32)
    if cuts:
        values = values * block_scale(own_key, extent, cuts, -0.22, 0.18)
    return jnp.clip(values, -bound, bound).astype(kind)


def noise_with(rng, dims, scale, bound, cuts, heavy, kind=jnp.bfloat16):
    entries = scale * jax.random.normal(rng, dims, jnp.float32)
    if cuts:
        entries = entries * block_scale(rng, dims, cuts, -0.22, 0.18)
    return jnp.clip(strengthened(entries, jax.random.fold_in(rng, 3), *heavy), -bound, bound).astype(kind)


def setup_inputs(seed: int = 0) -> dict:
    seeds = jax.random.split(jax.random.key(seed), 13)
    attn_inputs = noise_with(seeds[0], (ALLTOK, D), 1.0, 24.0, ((0, 512),), (0, 1, 512, 6.0))
    queries = draw_queries(jax.random.fold_in(seeds[12], 71), 0)
    key_vectors = draw_key_vectors(jax.random.fold_in(seeds[12], 71), 0)
    logp_grad = bell_draw(seeds[3], (ALLTOK, QH * HEAD), 4.0, 24.0, ((0, 512),))
    new_logp = draw_new_logp(jax.random.fold_in(seeds[12], 71), 0)
    old_logp = draw_old_logp(jax.random.fold_in(seeds[12], 71), 0)
    rewards = bell_draw(seeds[6], (ALLROLL,), 2.0, 8.0, (), jnp.float32)
    group_ids = with_ends(jax.random.randint(seeds[7], (ALLROLL,), 0, GROUPS), jax.random.fold_in(seeds[7], 1), 0, GROUPS - 1).astype(jnp.int32)
    lengths = with_ends(jax.random.randint(seeds[8], (ALLROLL,), LENGTH // 2, LENGTH + 1), jax.random.fold_in(seeds[8], 1), LENGTH // 2, LENGTH).astype(jnp.int32)
    value_proj = bell_draw(seeds[9], (D, KVH * HEAD), D ** -0.5, 0.078125, ((0, 32),))
    first_moment = bell_draw(seeds[10], (D, KVH * HEAD), 20.0, 120.0, ((0, 512),))
    second_moment = jnp.clip(jnp.exp(math.log(9984.0) - 4.603569 * jax.random.uniform(seeds[11], (D, KVH * HEAD), jnp.float32) ** block_scale(seeds[11], (D, KVH * HEAD), ((0, 512),), -0.2, 0.2)), 100.0, 9984.0).astype(jnp.bfloat16)
    return {"attn_inputs": attn_inputs, "queries": queries, "key_vectors": key_vectors, "logp_grad": logp_grad, "new_logp": new_logp, "old_logp": old_logp, "rewards": rewards, "group_ids": group_ids, "lengths": lengths, "value_proj": value_proj, "first_moment": first_moment, "second_moment": second_moment}


clip_low = 0.8
clip_high = 1.2
decay_first = 0.9
decay_second = 0.95
step_rate = 0.001
weight_decay = 0.1
adam_eps = 1e-08
bias_first = 1.0 - 0.9 ** 10
bias_second = 1.0 - 0.95 ** 10

def advantages(rewards, group_ids):
    group_count = rewards.shape[0] // 4
    member = (group_ids[:, None] == jnp.arange(group_count, dtype=jnp.int32)[None, :]).astype(jnp.float32)
    counts = jnp.maximum(lax.optimization_barrier(jnp.sum(member, axis=0)), 1.0)
    group_mean = lax.optimization_barrier(jnp.sum(member * rewards[:, None], axis=0)) / counts
    own_mean = lax.optimization_barrier(jnp.sum(member * group_mean[None, :], axis=1))
    spread = rewards - own_mean
    variance = lax.optimization_barrier(jnp.sum(member * (spread * spread)[:, None], axis=0)) / counts
    own_std = jnp.sqrt(lax.optimization_barrier(jnp.sum(member * variance[None, :], axis=1)))
    return spread / jnp.maximum(own_std, 1.0)

def coefficient(new_lp, old_lp, adv_tok, len_tok, pos_tok, full_len):
    ratio_now = jnp.exp(new_lp - old_lp)
    clipped = jnp.clip(ratio_now, clip_low, clip_high)
    active = (ratio_now * adv_tok <= clipped * adv_tok) & (pos_tok < len_tok)
    len_weight = full_len / len_tok.astype(jnp.float32)
    return jnp.where(active, -adv_tok * ratio_now * len_weight, 0.0)

def block_values(query_blk, grad_blk, roll_keys, first_pos):
    tok_rows = query_blk.shape[0]
    key_count = roll_keys.shape[0]
    per_group = QH // KVH
    score_scale = 1.0 / math.sqrt(HEAD)
    query_pos = first_pos + jnp.arange(tok_rows, dtype=jnp.int32)
    key_pos = jnp.arange(key_count, dtype=jnp.int32)
    allowed = jnp.tile(key_pos[None, :] <= query_pos[:, None], (per_group, 1))
    pieces = []
    for kv_head in range(KVH):
        col_low = kv_head * per_group * HEAD
        col_high = col_low + per_group * HEAD
        q_part = query_blk[:, col_low:col_high].reshape(tok_rows, per_group, HEAD).transpose(1, 0, 2).reshape(per_group * tok_rows, HEAD)
        g_part = grad_blk[:, col_low:col_high].reshape(tok_rows, per_group, HEAD).transpose(1, 0, 2).reshape(per_group * tok_rows, HEAD)
        k_part = roll_keys[:, kv_head * HEAD:(kv_head + 1) * HEAD]
        scores = jnp.dot(q_part, k_part.T, preferred_element_type=jnp.float32) * score_scale
        scores = jnp.where(allowed, scores, -1e+30)
        top_val = lax.optimization_barrier(jnp.max(scores, axis=1, keepdims=True))
        expo = jnp.exp(scores - top_val)
        attention = (expo / lax.optimization_barrier(jnp.sum(expo, axis=1, keepdims=True))).astype(jnp.bfloat16)
        pieces.append(jnp.dot(attention.T, g_part, preferred_element_type=jnp.float32))
    return jnp.concatenate(pieces, axis=1)

def adam_rows(old_rows, grad_rows, first_moment, second_moment):
    first = decay_first * first_moment.astype(jnp.float32) + (1.0 - decay_first) * grad_rows
    second = decay_second * second_moment.astype(jnp.float32) + (1.0 - decay_second) * grad_rows * grad_rows
    weight_now = old_rows.astype(jnp.float32)
    update = first / bias_first / (jnp.sqrt(second / bias_second) + adam_eps) + weight_decay * weight_now
    return ((weight_now - step_rate * update).astype(jnp.bfloat16), first.astype(jnp.bfloat16), second.astype(jnp.bfloat16))

def to_rollouts(array):
    half = TOK_DEV // ROLLS
    width = array.shape[1]
    shaped = array.reshape(N_SIDE, N_FSDP, ROLLS, half, width).transpose(0, 2, 1, 3, 4)
    return shaped.reshape(ALLROLL, N_FSDP, half, width)

def reference(attn_inputs, queries, key_vectors, logp_grad, new_logp, old_logp, rewards, group_ids, lengths, value_proj, first_moment, second_moment):
    half = TOK_DEV // ROLLS
    advantage = advantages(rewards, group_ids)
    token_ids = jnp.arange(ALLTOK, dtype=jnp.int32)
    copy_index = token_ids // TOKENS
    block_index = token_ids // TOK_DEV % N_FSDP
    slot = token_ids % TOK_DEV
    roll_index = copy_index * ROLLS + slot // half
    position = block_index * half + slot % half
    coeff = coefficient(new_logp, old_logp, advantage[roll_index], lengths[roll_index], position, LENGTH)
    out_grad = (coeff[:, None] * logp_grad.astype(jnp.float32)).astype(jnp.bfloat16)
    query_blocks = to_rollouts(queries)
    grad_blocks = to_rollouts(out_grad)
    keys_split = to_rollouts(key_vectors).reshape(ALLROLL, LENGTH, KVH * HEAD)

    def one_rollout(triple):
        query_roll, grad_roll, keys_roll = triple

        def add_block(running, block_in):
            query_blk, grad_blk, block_at = block_in
            partial_value = block_values(query_blk, grad_blk, keys_roll, block_at * half)
            rounded = lax.optimization_barrier(partial_value.astype(jnp.bfloat16))
            return (running + rounded.astype(jnp.float32), None)
        start_sum = jnp.zeros((LENGTH, KVH * HEAD), jnp.float32)
        running, _ = lax.scan(add_block, start_sum, (query_roll, grad_roll, jnp.arange(N_FSDP, dtype=jnp.int32)))
        return running.astype(jnp.bfloat16)
    rolled = lax.map(one_rollout, (query_blocks, grad_blocks, keys_split))
    values_grad = rolled.reshape(N_SIDE, ROLLS, N_FSDP, half, KVH * HEAD).transpose(0, 2, 1, 3, 4).reshape(ALLTOK, KVH * HEAD)
    input_grad = jnp.dot(values_grad, value_proj.T, preferred_element_type=jnp.float32).astype(jnp.bfloat16)
    weight_grad = jnp.dot(attn_inputs.T, values_grad, preferred_element_type=jnp.float32)
    new_proj, new_first, new_second = adam_rows(value_proj, weight_grad, first_moment, second_moment)
    return (input_grad, new_proj, new_first, new_second)
```

```python
import functools
import math

import jax
import jax.numpy as jnp
from jax import lax
from jax.experimental import pallas as pl
from jax.experimental.pallas import tpu as pltpu
from jax.sharding import Mesh
from jax.sharding import PartitionSpec as P

AXES = ("xl", "z", "y", "xh", "core")
FSDP = ("xl", "z")
SIDE = ("y", "xh", "core")
SIDE_FSDP = SIDE + FSDP
FSDP_SIDE = FSDP + SIDE
MESH = pl.DeviceIdType.MESH
NZ = 16
KVH = 4
PER = 5
HEAD = 128
QB = PER * 128
EXP_SCALE = math.log2(math.e) / math.sqrt(HEAD)
LOW = -1e30

clip_low = 0.8
clip_high = 1.2
decay_first = 0.9
decay_second = 0.95
step_rate = 0.001
weight_decay = 0.1
adam_eps = 1e-08
bias_first = 1.0 - 0.9**10
bias_second = 1.0 - 0.95**10


def coefficient_row(new_ref, old_ref, rew_ref, gid_ref, len_ref, side, first_pos):
    rew = rew_ref[...]
    gid = gid_ref[...]
    lens = len_ref[...]
    roll_of = lax.broadcasted_iota(jnp.int32, rew.shape, 1)
    adv_parts, len_parts = [], []
    for roll in range(2):
        own = roll_of == side * 2 + roll
        own_gid = jnp.sum(jnp.where(own, gid, 0), axis=1, keepdims=True)
        own_rew = jnp.sum(jnp.where(own, rew, 0.0), axis=1, keepdims=True)
        own_len = jnp.sum(jnp.where(own, lens, 0), axis=1, keepdims=True)
        member = jnp.where(gid == own_gid, 1.0, 0.0)
        count = jnp.maximum(jnp.sum(member, axis=1, keepdims=True), 1.0)
        mean = jnp.sum(member * rew, axis=1, keepdims=True) / count
        spread = rew - mean
        var = jnp.sum(member * (spread * spread), axis=1, keepdims=True) / count
        adv_parts.append((own_rew - mean) / jnp.maximum(jnp.sqrt(var), 1.0))
        len_parts.append(own_len)
    slot = lax.broadcasted_iota(jnp.int32, (1, 128), 1)
    first = slot < 64
    adv = jnp.where(first, adv_parts[0], adv_parts[1])
    length = jnp.where(first, len_parts[0], len_parts[1])
    pos = first_pos + jnp.where(first, slot, slot - 64)
    ratio = jnp.exp(new_ref[...] - old_ref[...])
    clipped = jnp.minimum(jnp.maximum(ratio, clip_low), clip_high)
    active = (ratio * adv <= clipped * adv) & (pos < length)
    return jnp.where(active, -adv * ratio * (2048.0 / length.astype(jnp.float32)), 0.0)


def attention_kernel(
    q_ref,
    g_ref,
    k_ref,
    new_ref,
    old_ref,
    rew_ref,
    gid_ref,
    len_ref,
    vg_ref,
    kbuf,
    gsend,
    qst,
    gst,
    qh,
    gh,
    eb,
    mst,
    mrow,
    lrow,
    pbuf,
    rsend,
    rrecv,
    vsend,
    x_send,
    x_recv,
    ag_send,
    ag_recv,
    rs_send,
    rs_recv,
):
    xl = lax.axis_index("xl")
    z = lax.axis_index("z")
    side = (lax.axis_index("y") * 2 + lax.axis_index("xh")) * 2 + lax.axis_index("core")
    up = lax.rem(z + 1, NZ)
    down = lax.rem(z + NZ - 1, NZ)
    mine = pl.ds(pl.multiple_of(64 * xl, 64), 64)
    theirs = pl.ds(pl.multiple_of(64 * (1 - xl), 64), 64)

    barrier = pltpu.get_barrier_semaphore()
    pl.semaphore_signal(barrier, inc=1, device_id={"xl": 1 - xl}, device_id_type=MESH)
    pl.semaphore_signal(barrier, inc=1, device_id={"z": up}, device_id_type=MESH)
    pl.semaphore_signal(barrier, inc=1, device_id={"z": down}, device_id_type=MESH)
    kbuf[z, xl] = k_ref[mine, :]
    pl.semaphore_wait(barrier, 3)

    def pair_copy(src, dst, at):
        return pltpu.make_async_remote_copy(
            src_ref=src,
            dst_ref=dst,
            send_sem=x_send.at[at],
            recv_sem=x_recv.at[at],
            device_id={"xl": 1 - xl},
            device_id_type=MESH,
        )

    def ring(way):
        return {"z": up if way == 0 else down}

    def key_copy(way, step, half):
        back = step - 1
        block = lax.rem(z + NZ - back, NZ) if way == 0 else lax.rem(z + back, NZ)
        return pltpu.make_async_remote_copy(
            src_ref=kbuf.at[block, half],
            dst_ref=kbuf.at[block, half],
            send_sem=ag_send.at[way, back, half],
            recv_sem=ag_recv.at[way, back, half],
            device_id=ring(way),
            device_id_type=MESH,
        )

    def part_copy(way, step, half):
        return pltpu.make_async_remote_copy(
            src_ref=rsend.at[way, step, half],
            dst_ref=rrecv.at[way, step, half],
            send_sem=rs_send.at[way, step, half],
            recv_sem=rs_recv.at[way, step, half],
            device_id=ring(way),
            device_id_type=MESH,
        )

    key_pair = pair_copy(k_ref.at[theirs], kbuf.at[z, xl], 0)
    query_pair = pair_copy(q_ref.at[theirs], qst, 1)
    grad_pair = pair_copy(gsend.at[theirs], gst, 2)
    key_pair.start()
    for way in range(2):
        key_copy(way, 1, xl).start()
    query_pair.start()

    coeff = coefficient_row(
        new_ref, old_ref, rew_ref, gid_ref, len_ref, side, (xl * NZ + z) * 64
    )
    diag = lax.broadcasted_iota(jnp.int32, (128, 128), 0) == lax.broadcasted_iota(
        jnp.int32, (128, 128), 1
    )
    coeff_col = jnp.sum(jnp.where(diag, coeff, 0.0), axis=1, keepdims=True)
    for head in range(KVH * PER):
        cols = slice(head * HEAD, (head + 1) * HEAD)
        gsend[:, cols] = (coeff_col * g_ref[:, cols].astype(jnp.float32)).astype(jnp.bfloat16)
    grad_pair.start()

    key_pair.wait_recv()
    for way in range(2):
        key_copy(way, 1, 1 - xl).start()

    def spread(dst, src, rows, half):
        for head in range(KVH * PER):
            at = pl.ds(pl.multiple_of(64 * half, 64) + (head % PER) * 128, 64)
            dst[head // PER, at, :] = src[rows, head * HEAD : (head + 1) * HEAD]

    spread(qh, q_ref, mine, xl)
    spread(gh, gsend, mine, xl)
    mrow[...] = jnp.full(mrow.shape, LOW, jnp.float32)
    lrow[...] = jnp.zeros(lrow.shape, jnp.float32)

    def arrived(step):
        for way in range(2):
            if way == 1 and step == 8:
                continue
            for half in range(2):
                key_copy(way, step, half).wait_recv()
                if step < (8 if way == 0 else 7):
                    key_copy(way, step + 1, half).start()

    row = lax.broadcasted_iota(jnp.int32, (256, 1), 0)
    lane = lax.broadcasted_iota(jnp.int32, (1, QB), 1)
    in_head = lax.rem(lane, 128)
    qpos = jnp.where(in_head < 64, in_head, in_head - 64 + 1024) + z * 64
    in_block = lax.rem(row, 128)
    kpos_base = jnp.where(in_block < 64, in_block, in_block - 64 + 1024)

    def score(index, carry):
        t = index // KVH + 1
        head = lax.rem(index, KVH)
        cols = pl.ds(pl.multiple_of(head * HEAD, HEAD), HEAD)
        a = lax.rem(z + NZ - t, NZ)
        b = lax.rem(z + jnp.where(t == 8, 0, t), NZ)
        keys = jnp.concatenate(
            [
                kbuf[a, :, :, cols].reshape(128, HEAD),
                kbuf[b, :, :, cols].reshape(128, HEAD),
            ],
            axis=0,
        )
        s = lax.dot_general(
            keys, qh[head], (((1,), (1,)), ((), ())), preferred_element_type=jnp.float32
        )
        kpos = kpos_base + jnp.where(row < 128, a, b) * 64
        s = jnp.where(kpos <= qpos, s, LOW)
        old = mrow[head]
        top = jnp.maximum(old, jnp.max(s, axis=0, keepdims=True))
        e = jnp.exp2((s - top) * EXP_SCALE)
        lrow[head] = lrow[head] * jnp.exp2((old - top) * EXP_SCALE) + jnp.sum(
            e, axis=0, keepdims=True
        )
        mrow[head] = top
        mst[t - 1, head] = top
        eb[t - 1, head] = e.astype(jnp.bfloat16)
        return carry

    def scores(first, last):
        lax.fori_loop((first - 1) * KVH, last * KVH, score, 0)

    for step in range(1, 4):
        arrived(step)
    query_pair.wait_recv()
    spread(qh, qst, slice(None), 1 - xl)
    arrived(4)
    scores(1, 2)
    arrived(5)
    scores(3, 4)
    arrived(6)
    scores(5, 5)
    arrived(7)
    scores(6, 7)
    grad_pair.wait_recv()
    spread(gh, gst, slice(None), 1 - xl)
    arrived(8)
    scores(8, 8)

    def part(t, which, slot):
        def one(head, carry):
            cols = pl.ds(pl.multiple_of(head * HEAD, HEAD), HEAD)
            scale = jnp.exp2((mst[t - 1, head] - mrow[head]) * EXP_SCALE) / lrow[head]
            p = eb[t - 1, head, pl.ds(which * 128, 128), :].astype(jnp.float32) * scale
            pbuf[slot, :, cols] = jnp.dot(
                p.astype(jnp.bfloat16), gh[head], preferred_element_type=jnp.float32
            )
            return carry

        lax.fori_loop(0, KVH, one, 0)

    def pass_on(way, step):
        for half in range(2):
            value = pbuf[way, half * 64 : (half + 1) * 64, :]
            if step > 0:
                part_copy(way, step - 1, half).wait_recv()
                value = value + rrecv[way, step - 1, half].astype(jnp.float32)
            rsend[way, step, half] = value.astype(jnp.bfloat16)
            part_copy(way, step, half).start()

    for step in range(8):
        part(8 - step, 0 if step == 0 else 1, 0)
        pass_on(0, step)
        if step < 7:
            part(7 - step, 0, 1)
            pass_on(1, step)
    part(8, 1, 0)
    value_pair = pair_copy(vsend, vg_ref.at[pl.ds(pl.multiple_of(64 * xl, 64), 64)], 3)
    for half in range(2):
        part_copy(1, 6, half).wait_recv()
        part_copy(0, 7, half).wait_recv()
    own = pl.ds(pl.multiple_of(64 * xl, 64), 64)
    other = pl.ds(pl.multiple_of(64 * (1 - xl), 64), 64)
    vsend[...] = (
        pbuf[0, other, :]
        + rrecv[1, 6, 1 - xl].astype(jnp.float32)
        + rrecv[0, 7, 1 - xl].astype(jnp.float32)
    ).astype(jnp.bfloat16)
    value_pair.start()
    vg_ref[own, :] = (
        pbuf[0, own, :]
        + rrecv[1, 6, xl].astype(jnp.float32)
        + rrecv[0, 7, xl].astype(jnp.float32)
    ).astype(jnp.bfloat16)
    for way in range(2):
        for step in range(8 - way):
            for half in range(2):
                key_copy(way, step + 1, half).wait_send()
                part_copy(way, step, half).wait_send()
    key_pair.wait_send()
    query_pair.wait_send()
    grad_pair.wait_send()
    value_pair.wait()


def value_gradients(queries, logp_grad, key_vectors, new_logp, old_logp, rewards, gids, lengths):
    vmem = pl.BlockSpec(memory_space=pltpu.VMEM)
    dma = pltpu.SemaphoreType.DMA
    bf, f32 = jnp.bfloat16, jnp.float32
    return pl.pallas_call(
        attention_kernel,
        out_shape=jax.ShapeDtypeStruct((128, 512), bf),
        in_specs=[vmem] * 8,
        out_specs=vmem,
        scratch_shapes=[
            pltpu.VMEM((NZ, 2, 64, 512), bf),
            pltpu.VMEM((128, 2560), bf),
            pltpu.VMEM((64, 2560), bf),
            pltpu.VMEM((64, 2560), bf),
            pltpu.VMEM((KVH, QB, HEAD), bf),
            pltpu.VMEM((KVH, QB, HEAD), bf),
            pltpu.VMEM((8, KVH, 256, QB), bf),
            pltpu.VMEM((8, KVH, 1, QB), f32),
            pltpu.VMEM((KVH, 1, QB), f32),
            pltpu.VMEM((KVH, 1, QB), f32),
            pltpu.VMEM((2, 128, 512), f32),
            pltpu.VMEM((2, 8, 2, 64, 512), bf),
            pltpu.VMEM((2, 8, 2, 64, 512), bf),
            pltpu.VMEM((64, 512), bf),
            dma((4,)),
            dma((4,)),
            dma((2, 8, 2)),
            dma((2, 8, 2)),
            dma((2, 8, 2)),
            dma((2, 8, 2)),
        ],
        compiler_params=pltpu.CompilerParams(
            collective_id=0, has_side_effects=True, vmem_limit_bytes=48 * 1024 * 1024
        ),
    )(
        queries,
        logp_grad,
        key_vectors,
        new_logp.reshape(1, 128),
        old_logp.reshape(1, 128),
        rewards.reshape(1, 32),
        gids.reshape(1, 32),
        lengths.reshape(1, 32),
    )


def split_up(value, dim, peers):
    before, after = (value.shape[:dim], value.shape[dim + 1 :])
    return jnp.moveaxis(value.reshape(*before, peers, -1, *after), dim, 0)


def laid_out(pieces, dim):
    pieces = jnp.moveaxis(pieces, 0, dim)
    dims = pieces.shape
    return pieces.reshape(*dims[:dim], dims[dim] * dims[dim + 1], *dims[dim + 2 :])


def sum_at_owner(value, axis, dim):
    pieces = split_up(value, dim, lax.axis_size(axis))
    arrived = lax.all_to_all(pieces, axis, split_axis=0, concat_axis=0, tiled=True)
    return arrived.astype(jnp.float32).sum(axis=0)


def collect(value, axis, dim):
    peers = lax.axis_size(axis)
    pieces = lax.all_to_all(
        jnp.broadcast_to(value[None], (peers, *value.shape)), axis, 0, 0, tiled=True
    )
    return laid_out(pieces, dim)


def adam_rows(old_rows, grad_rows, first_moment, second_moment):
    first = decay_first * first_moment.astype(jnp.float32) + (1.0 - decay_first) * grad_rows
    second = (
        decay_second * second_moment.astype(jnp.float32)
        + (1.0 - decay_second) * grad_rows * grad_rows
    )
    weight_now = old_rows.astype(jnp.float32)
    update = (
        first / bias_first / (jnp.sqrt(second / bias_second) + adam_eps) + weight_decay * weight_now
    )
    return (
        (weight_now - step_rate * update).astype(jnp.bfloat16),
        first.astype(jnp.bfloat16),
        second.astype(jnp.bfloat16),
    )


def shards(
    attn_inputs,
    queries,
    key_vectors,
    logp_grad,
    new_logp,
    old_logp,
    rewards,
    group_ids,
    lengths,
    value_proj,
    first_moment,
    second_moment,
):
    side_index = lax.axis_index(SIDE)
    own_grad = value_gradients(
        queries, logp_grad, key_vectors, new_logp, old_logp, rewards, group_ids, lengths
    )
    in_columns = lax.all_to_all(attn_inputs, FSDP, split_axis=1, concat_axis=0, tiled=True)
    values_grad = lax.all_gather(own_grad, FSDP, axis=0, tiled=True)
    weights = lax.all_gather(value_proj, FSDP, axis=0, tiled=True)
    input_grad = jnp.dot(own_grad, weights.T, preferred_element_type=jnp.float32).astype(
        jnp.bfloat16
    )
    weight_grad = lax.dot_general(
        in_columns, values_grad, (((0,), (0,)), ((), ())), preferred_element_type=jnp.float32
    )
    shard_grad = sum_at_owner(weight_grad.astype(jnp.bfloat16), SIDE, 0)
    shard_rows = shard_grad.shape[0]
    old_rows = lax.dynamic_slice_in_dim(value_proj, side_index * shard_rows, shard_rows, 0)
    new_rows, new_first, new_second = adam_rows(old_rows, shard_grad, first_moment, second_moment)
    new_proj = collect(new_rows, SIDE, 0)
    return (input_grad, new_proj, new_first, new_second)


def solution(mesh):
    torus = Mesh(mesh.devices.reshape(2, 16, 4, 2, 2), AXES)
    placed = (
        P(SIDE_FSDP, None),
        P(SIDE_FSDP, None),
        P(SIDE_FSDP, None),
        P(SIDE_FSDP, None),
        P(SIDE_FSDP),
        P(SIDE_FSDP),
        P(),
        P(),
        P(),
        P(FSDP, None),
        P(FSDP_SIDE, None),
        P(FSDP_SIDE, None),
    )
    return jax.shard_map(
        shards,
        mesh=torus,
        in_specs=placed,
        out_specs=(P(SIDE_FSDP, None), P(FSDP, None), P(FSDP_SIDE, None), P(FSDP_SIDE, None)),
        check_vma=False,
    )
```

```python
import math

import jax
import jax.numpy as jnp
from jax import lax
from jax.experimental import pallas as pl
from jax.experimental.pallas import tpu as pltpu
from jax.sharding import Mesh
from jax.sharding import PartitionSpec as P

AXES = ("xl", "z", "y", "xh", "core")
FSDP = ("xl", "z")
SIDE = ("y", "xh", "core")
SIDE_FSDP = SIDE + FSDP
FSDP_SIDE = FSDP + SIDE
MESH = pl.DeviceIdType.MESH
NZ = 16
KVH = 4
PER = 5
HEAD = 128
QB = PER * 128
EXP_SCALE = math.log2(math.e) / math.sqrt(HEAD)
LOW = -1e30

clip_low = 0.8
clip_high = 1.2
decay_first = 0.9
decay_second = 0.95
step_rate = 0.001
weight_decay = 0.1
adam_eps = 1e-08
bias_first = 1.0 - 0.9**10
bias_second = 1.0 - 0.95**10


def coefficient_row(new_ref, old_ref, rew_ref, gid_ref, len_ref, side, first_pos):
    rew = rew_ref[...]
    gid = gid_ref[...]
    lens = len_ref[...]
    roll_of = lax.broadcasted_iota(jnp.int32, rew.shape, 1)
    adv_parts, len_parts = [], []
    for roll in range(2):
        own = roll_of == side * 2 + roll
        own_gid = jnp.sum(jnp.where(own, gid, 0), axis=1, keepdims=True)
        own_rew = jnp.sum(jnp.where(own, rew, 0.0), axis=1, keepdims=True)
        own_len = jnp.sum(jnp.where(own, lens, 0), axis=1, keepdims=True)
        member = jnp.where(gid == own_gid, 1.0, 0.0)
        count = jnp.maximum(jnp.sum(member, axis=1, keepdims=True), 1.0)
        mean = jnp.sum(member * rew, axis=1, keepdims=True) / count
        spread = rew - mean
        var = jnp.sum(member * (spread * spread), axis=1, keepdims=True) / count
        adv_parts.append((own_rew - mean) / jnp.maximum(jnp.sqrt(var), 1.0))
        len_parts.append(own_len)
    slot = lax.broadcasted_iota(jnp.int32, (1, 128), 1)
    first = slot < 64
    adv = jnp.where(first, adv_parts[0], adv_parts[1])
    length = jnp.where(first, len_parts[0], len_parts[1])
    pos = first_pos + jnp.where(first, slot, slot - 64)
    ratio = jnp.exp(new_ref[...] - old_ref[...])
    clipped = jnp.minimum(jnp.maximum(ratio, clip_low), clip_high)
    active = (ratio * adv <= clipped * adv) & (pos < length)
    return jnp.where(active, -adv * ratio * (2048.0 / length.astype(jnp.float32)), 0.0)


def adam_rows(weight_now, grad_rows, first_moment, second_moment):
    first = decay_first * first_moment + (1.0 - decay_first) * grad_rows
    second = decay_second * second_moment + (1.0 - decay_second) * grad_rows * grad_rows
    update = (
        first / bias_first / (jnp.sqrt(second / bias_second) + adam_eps) + weight_decay * weight_now
    )
    return weight_now - step_rate * update, first, second


def kernel(
    x_hbm,
    q_hbm,
    k_hbm,
    g_hbm,
    new_hbm,
    old_hbm,
    rew_hbm,
    gid_hbm,
    len_hbm,
    w_hbm,
    m1_ref,
    m2_ref,
    ig_ref,
    np_ref,
    nf_ref,
    ns_ref,
    qv,
    gv,
    kv,
    xv,
    wv,
    newv,
    oldv,
    rewv,
    gidv,
    lenv,
    kbuf,
    gsend,
    qst,
    gst,
    qh,
    gh,
    eb,
    mst,
    mrow,
    lrow,
    pbuf,
    rsend,
    rrecv,
    vsend,
    vrecv,
    xt,
    xg,
    wfull,
    mv,
    moms,
    m1f,
    m2f,
    vga,
    acc,
    xs,
    xr,
    zsum,
    zs,
    zr,
    gy,
    gf,
    load_sem,
    x_send,
    x_recv,
    ag_send,
    ag_recv,
    rs_send,
    rs_recv,
    in_send,
    in_recv,
    wz_send,
    wz_recv,
    wy_send,
    wy_recv,
    mo_send,
    mo_recv,
    va_send,
    va_recv,
    xs_send,
    xs_recv,
    zs_send,
    zs_recv,
    gy_send,
    gy_recv,
    gf_send,
    gf_recv,
):
    xl = lax.axis_index("xl")
    z = lax.axis_index("z")
    y = lax.axis_index("y")
    xh = lax.axis_index("xh")
    core = lax.axis_index("core")
    side = (y * 2 + xh) * 2 + core
    x = xh * 2 + xl
    up = lax.rem(z + 1, NZ)
    down = lax.rem(z + NZ - 1, NZ)
    mine = pl.ds(pl.multiple_of(64 * xl, 64), 64)
    theirs = pl.ds(pl.multiple_of(64 * (1 - xl), 64), 64)

    def lanes(index):
        return pl.ds(pl.multiple_of(index * 128, 128), 128)

    def y_at(step):
        return lax.rem(y + step, 4)

    loads = [
        pltpu.make_async_copy(src, dst, load_sem.at[i])
        for i, (src, dst) in enumerate(
            (
                (k_hbm, kv),
                (q_hbm, qv),
                (w_hbm, wv),
                (new_hbm, newv),
                (old_hbm, oldv),
                (rew_hbm, rewv),
                (gid_hbm, gidv),
                (len_hbm, lenv),
                (g_hbm, gv),
                (x_hbm, xv),
            )
        )
    ]
    for load in loads:
        load.start()

    barrier = pltpu.get_barrier_semaphore()

    def greet(**where):
        pl.semaphore_signal(barrier, inc=1, device_id=where, device_id_type=MESH)

    for step in range(1, NZ):
        greet(z=lax.rem(z + step, NZ))
    for flip in range(1, 8):
        greet(xl=xl ^ (flip & 1), xh=xh ^ (flip >> 1 & 1), core=core ^ (flip >> 2))
    for step in range(1, 4):
        for flip in range(4):
            greet(y=y_at(step), xh=xh ^ (flip & 1), core=core ^ (flip >> 1))

    mv[...] = jnp.zeros(mv.shape, mv.dtype)
    mv[0:10, :] = m1_ref[...]
    mv[16:26, :] = m2_ref[...]
    moms[side] = mv[...]
    loads[0].wait()
    kbuf[z, xl] = kv[mine, :]
    for i in range(1, 3):
        loads[i].wait()
    pl.semaphore_wait(barrier, NZ - 1 + 7 + 12)

    def copy_to(src, dst, send, recv, **where):
        return pltpu.make_async_remote_copy(
            src_ref=src,
            dst_ref=dst,
            send_sem=send,
            recv_sem=recv,
            device_id=where,
            device_id_type=MESH,
        )

    def pair_copy(src, dst, at):
        return copy_to(src, dst, x_send.at[at], x_recv.at[at], xl=1 - xl)

    def ring_block(way, step):
        back = step - 1
        return lax.rem(z + NZ - back, NZ) if way == 0 else lax.rem(z + back, NZ)

    def key_copy(way, step, half):
        part = kbuf.at[ring_block(way, step), half]
        return copy_to(
            part,
            part,
            ag_send.at[way, step - 1, half],
            ag_recv.at[way, step - 1, half],
            z=up if way == 0 else down,
        )

    def weight_copy(way, step):
        part = wfull.at[core * NZ + ring_block(way, step), :, lanes(y)]
        return copy_to(
            part,
            part,
            wz_send.at[way, step - 1],
            wz_recv.at[way, step - 1],
            z=up if way == 0 else down,
        )

    def part_copy(way, step, half):
        return copy_to(
            rsend.at[way, step, half],
            rrecv.at[way, step, half],
            rs_send.at[way, step, half],
            rs_recv.at[way, step, half],
            z=up if way == 0 else down,
        )

    key_pair = pair_copy(kv.at[theirs], kbuf.at[z, xl], 0)
    query_pair = pair_copy(qv.at[theirs], qst, 1)
    grad_pair = pair_copy(gsend.at[theirs], gst, 2)
    own_weight = wfull.at[core * NZ + z, :, lanes(y)]
    weight_pair = pair_copy(wv.at[:, lanes(y)], own_weight, 3)
    key_pair.start()
    for way in range(2):
        key_copy(way, 1, xl).start()

    @pl.when(core == xl)
    def _():
        weight_pair.start()
        wfull[core * NZ + z, :, lanes(y)] = wv[:, lanes(y)]

    query_pair.start()

    for i in range(3, 9):
        loads[i].wait()
    coeff = coefficient_row(newv, oldv, rewv, gidv, lenv, side, (xl * NZ + z) * 64)
    diag = lax.broadcasted_iota(jnp.int32, (128, 128), 0) == lax.broadcasted_iota(
        jnp.int32, (128, 128), 1
    )
    coeff_col = jnp.sum(jnp.where(diag, coeff, 0.0), axis=1, keepdims=True)
    for head in range(KVH * PER):
        cols = slice(head * HEAD, (head + 1) * HEAD)
        gsend[:, cols] = (coeff_col * gv[:, cols].astype(jnp.float32)).astype(jnp.bfloat16)
    grad_pair.start()

    key_pair.wait_recv()
    for way in range(2):
        key_copy(way, 1, 1 - xl).start()

    @pl.when(core != xl)
    def _():
        weight_pair.wait_recv()

    for way in range(2):
        weight_copy(way, 1).start()

    def spread(dst, src, rows, half):
        for head in range(KVH * PER):
            at = pl.ds(pl.multiple_of(64 * half, 64) + (head % PER) * 128, 64)
            dst[head // PER, at, :] = src[rows, head * HEAD : (head + 1) * HEAD]

    spread(qh, qv, mine, xl)
    spread(gh, gsend, mine, xl)
    mrow[...] = jnp.full(mrow.shape, LOW, jnp.float32)
    lrow[...] = jnp.zeros(lrow.shape, jnp.float32)

    def arrived(step):
        for half in range(2):
            for way in range(2):
                if way == 1 and step == 8:
                    continue
                key_copy(way, step, half).wait_recv()
                if step < 8 - way:
                    key_copy(way, step + 1, half).start()
        for way in range(2):
            if way == 1 and step == 8:
                continue
            weight_copy(way, step).wait_recv()
            if step < 8 - way:
                weight_copy(way, step + 1).start()

    loads[9].wait()

    def turn(n, carry):
        cols = pl.ds(pl.multiple_of(n * 640, 128), 640)
        xt[n] = xv[:, cols].T.reshape(4, 160, 128)
        return carry

    def input_copies():
        copies = []
        for step in range(4):
            for flip in range(2):
                if step + flip:
                    there = core ^ flip
                    copies.append(
                        copy_to(
                            xt.at[pl.ds(4 * there, 4), y_at(step)],
                            xg.at[:, :, lanes(2 * y + core)],
                            in_send.at[step * 2 + flip],
                            in_recv.at[step * 2 + flip],
                            y=y_at(step),
                            core=there,
                        )
                    )
        return copies

    def moment_copies():
        copies = []
        for step in range(4):
            for flip in range(4):
                if step + flip:
                    copies.append(
                        copy_to(
                            mv,
                            moms.at[side],
                            mo_send.at[step * 4 + flip],
                            mo_recv.at[step * 4 + flip],
                            y=y_at(step),
                            xh=xh ^ (flip & 1),
                            core=core ^ (flip >> 1),
                        )
                    )
        return copies

    row = lax.broadcasted_iota(jnp.int32, (256, 1), 0)
    lane = lax.broadcasted_iota(jnp.int32, (1, QB), 1)
    in_head = lax.rem(lane, 128)
    qpos = jnp.where(in_head < 64, in_head, in_head - 64 + 1024) + z * 64
    in_block = lax.rem(row, 128)
    kpos_base = jnp.where(in_block < 64, in_block, in_block - 64 + 1024)

    def score(index, carry):
        t = index // KVH + 1
        head = lax.rem(index, KVH)
        a = lax.rem(z + NZ - t, NZ)
        b = lax.rem(z + jnp.where(t == 8, 0, t), NZ)
        keys = jnp.concatenate(
            [
                kbuf[a, :, :, lanes(head)].reshape(128, HEAD),
                kbuf[b, :, :, lanes(head)].reshape(128, HEAD),
            ],
            axis=0,
        )
        s = lax.dot_general(
            keys, qh[head], (((1,), (1,)), ((), ())), preferred_element_type=jnp.float32
        )
        kpos = kpos_base + jnp.where(row < 128, a, b) * 64
        s = jnp.where(kpos <= qpos, s, LOW)
        old = mrow[head]
        top = jnp.maximum(old, jnp.max(s, axis=0, keepdims=True))
        e = jnp.exp2((s - top) * EXP_SCALE)
        lrow[head] = lrow[head] * jnp.exp2((old - top) * EXP_SCALE) + jnp.sum(
            e, axis=0, keepdims=True
        )
        mrow[head] = top
        mst[t - 1, head] = top
        eb[t - 1, head] = e.astype(jnp.bfloat16)
        return carry

    def scores(first, last):
        lax.fori_loop((first - 1) * KVH, last * KVH, score, 0)

    arrived(1)
    lax.fori_loop(0, 4, turn, 0)
    arrived(2)
    lax.fori_loop(4, 8, turn, 0)
    xg[:, :, lanes(2 * y + core)] = xt[pl.ds(4 * core, 4), y]
    for copy in input_copies():
        copy.start()
    arrived(3)
    for copy in moment_copies():
        copy.start()
    query_pair.wait_recv()
    spread(qh, qst, slice(None), 1 - xl)
    arrived(4)
    scores(1, 2)
    arrived(5)
    scores(3, 4)
    arrived(6)
    scores(5, 5)
    arrived(7)
    scores(6, 7)
    grad_pair.wait_recv()
    spread(gh, gst, slice(None), 1 - xl)
    arrived(8)

    def across_y(step):
        part = wfull.at[pl.ds(NZ * core, NZ), :, lanes(y)]
        return copy_to(part, part, wy_send.at[step], wy_recv.at[step], y=y_at(step))

    def across_core():
        part = wfull.at[pl.ds(NZ * core, NZ)]
        return copy_to(part, part, wy_send.at[0], wy_recv.at[0], core=1 - core)

    for step in range(1, 4):
        across_y(step).start()
    scores(8, 8)

    def part(t, which, slot):
        def one(head, carry):
            scale = jnp.exp2((mst[t - 1, head] - mrow[head]) * EXP_SCALE) / lrow[head]
            p = eb[t - 1, head, pl.ds(which * 128, 128), :].astype(jnp.float32) * scale
            pbuf[slot, :, lanes(head)] = jnp.dot(
                p.astype(jnp.bfloat16), gh[head], preferred_element_type=jnp.float32
            )
            return carry

        lax.fori_loop(0, KVH, one, 0)

    def pass_on(way, step):
        for half in range(2):
            value = pbuf[way, half * 64 : (half + 1) * 64, :]
            if step > 0:
                part_copy(way, step - 1, half).wait_recv()
                value = value + rrecv[way, step - 1, half].astype(jnp.float32)
            rsend[way, step, half] = value.astype(jnp.bfloat16)
            part_copy(way, step, half).start()

    for step in range(8):
        part(8 - step, 0 if step == 0 else 1, 0)
        pass_on(0, step)
        if step < 7:
            part(7 - step, 0, 1)
            pass_on(1, step)
    part(8, 1, 0)

    for copy in moment_copies():
        copy.wait_recv()
    for s in range(16):
        m1f[10 * s : 10 * s + 10, :] = moms[s, 0:10, :].astype(jnp.float32)
        m2f[10 * s : 10 * s + 10, :] = moms[s, 16:26, :].astype(jnp.float32)

    value_pair = pair_copy(vsend, vrecv, 4)
    for half in range(2):
        part_copy(1, 6, half).wait_recv()
        part_copy(0, 7, half).wait_recv()
    vsend[...] = (
        pbuf[0, theirs, :]
        + rrecv[1, 6, 1 - xl].astype(jnp.float32)
        + rrecv[0, 7, 1 - xl].astype(jnp.float32)
    ).astype(jnp.bfloat16)
    value_pair.start()
    slot = 2 * y + core
    vga[slot, mine, :] = (
        pbuf[0, mine, :]
        + rrecv[1, 6, xl].astype(jnp.float32)
        + rrecv[0, 7, xl].astype(jnp.float32)
    ).astype(jnp.bfloat16)
    value_pair.wait_recv()
    vga[slot, theirs, :] = vrecv[...]

    def values_y(step):
        return copy_to(vga.at[slot], vga.at[slot], va_send.at[step], va_recv.at[step], y=y_at(step))

    def values_core(step):
        part = vga.at[2 * lax.rem(y + 4 - step, 4) + core]
        return copy_to(part, part, va_send.at[4 + step], va_recv.at[4 + step], core=1 - core)

    for step in (2, 1, 3):
        values_y(step).start()
    values_core(0).start()

    for copy in input_copies():
        copy.wait_recv()
    for step in range(1, 4):
        across_y(step).wait_recv()
    across_core().start()

    def add_inputs(step, first):
        at = lax.rem(y + 4 - step, 4)
        a = xg[:, :, pl.ds(pl.multiple_of(at * 256, 256), 256)].reshape(640, 256)
        b = vga[pl.ds(2 * at, 2)].reshape(256, 512)
        value = jnp.dot(a, b, preferred_element_type=jnp.float32)
        acc[...] = value if first else acc[...] + value

    values_core(0).wait_recv()
    add_inputs(0, True)
    for step in (1, 3, 2):
        values_y(step).wait_recv()
        values_core(step).start()
        values_core(step).wait_recv()
        add_inputs(step, False)

    def sum_x(step):
        at = lax.rem(x + step, 4)
        return copy_to(
            xs.at[step - 1],
            xr.at[step - 1],
            xs_send.at[step - 1],
            xs_recv.at[step - 1],
            xl=lax.rem(at, 2),
            xh=at // 2,
        )

    for step in (2, 1, 3):
        at = lax.rem(x + step, 4)
        xs[step - 1] = acc[:, lanes(at)].astype(jnp.bfloat16)
        sum_x(step).start()

    across_core().wait_recv()

    def grad_tile(n, carry):
        w = wfull[pl.ds(4 * n, 4)].reshape(640, 512)
        ig_ref[:, pl.ds(pl.multiple_of(n * 640, 128), 640)] = lax.dot_general(
            vga[slot], w, (((1,), (1,)), ((), ())), preferred_element_type=jnp.float32
        ).astype(jnp.bfloat16)
        return carry

    lax.fori_loop(0, 8, grad_tile, 0)

    for step in (1, 3, 2):
        sum_x(step).wait_recv()
    total = acc[:, lanes(x)]
    for step in range(3):
        total = total + xr[step].astype(jnp.float32)
    zsum[...] = total.reshape(4, 160, 128)
    zs[...] = zsum[...].astype(jnp.bfloat16)

    def sum_z(j):
        at = 4 * j + y
        far = lax.rem(z - at + NZ, NZ)
        return copy_to(zs.at[j], zr.at[far], zs_send.at[j], zs_recv.at[far], z=at)

    for j in range(4):

        @pl.when(z != 4 * j + y)
        def _(j=j):
            sum_z(j).start()

    root = lax.rem(z, 4) == y

    def spread_y(step):
        return copy_to(gy, gy, gy_send.at[step - 1], gy_recv, y=y_at(step))

    @pl.when(root)
    def _():
        total = zsum[z // 4]
        for far in range(1, NZ):
            copy_to(zs.at[0], zr.at[far], zs_send.at[0], zs_recv.at[far], z=up).wait_recv()
            total = total + zr[far].astype(jnp.float32)
        gy[...] = total.astype(jnp.bfloat16)
        for step in range(1, 4):
            spread_y(step).start()

    @pl.when(jnp.logical_not(root))
    def _():
        spread_y(1).wait_recv()

    def spread_x(to_xh, to_core):
        k = to_xh * 2 + to_core
        return copy_to(
            gy, gf.at[x], gf_send.at[k], gf_recv.at[x], xl=core, xh=to_xh, core=to_core
        )

    def is_self(to_xh, to_core):
        return (xl == core) & (xh == to_xh) & (core == to_core)

    for to_xh in range(2):
        for to_core in range(2):

            @pl.when(jnp.logical_not(is_self(to_xh, to_core)))
            def _(to_xh=to_xh, to_core=to_core):
                spread_x(to_xh, to_core).start()

    @pl.when(xl == core)
    def _():
        gf[x] = gy[...]

    for at in range(4):

        @pl.when(jnp.logical_not((xl == core) & (x == at)))
        def _(at=at):
            copy_to(gy, gf.at[at], gf_send.at[0], gf_recv.at[at], core=1 - core).wait_recv()

    for at in range(4):
        cols = slice(at * 128, (at + 1) * 128)
        new, first, second = adam_rows(
            wv[:, cols].astype(jnp.float32),
            gf[at].astype(jnp.float32),
            m1f[:, cols],
            m2f[:, cols],
        )
        np_ref[:, cols] = new.astype(jnp.bfloat16)
        m1f[:, cols] = first
        m2f[:, cols] = second
    for s in range(16):

        @pl.when(side == s)
        def _(s=s):
            nf_ref[...] = m1f[10 * s : 10 * s + 10, :].astype(jnp.bfloat16)
            ns_ref[...] = m2f[10 * s : 10 * s + 10, :].astype(jnp.bfloat16)

    for way in range(2):
        for step in range(8 - way):
            weight_copy(way, step + 1).wait_send()
            for half in range(2):
                key_copy(way, step + 1, half).wait_send()
                part_copy(way, step, half).wait_send()
    for copy in (key_pair, query_pair, grad_pair, value_pair):
        copy.wait_send()

    @pl.when(core == xl)
    def _():
        weight_pair.wait_send()

    for copy in input_copies() + moment_copies():
        copy.wait_send()
    across_core().wait_send()
    values_core(0).wait_send()
    for step in range(1, 4):
        across_y(step).wait_send()
        values_y(step).wait_send()
        values_core(step).wait_send()
        sum_x(step).wait_send()
    for j in range(4):

        @pl.when(z != 4 * j + y)
        def _(j=j):
            sum_z(j).wait_send()

    @pl.when(root)
    def _():
        for step in range(1, 4):
            spread_y(step).wait_send()

    for to_xh in range(2):
        for to_core in range(2):

            @pl.when(jnp.logical_not(is_self(to_xh, to_core)))
            def _(to_xh=to_xh, to_core=to_core):
                spread_x(to_xh, to_core).wait_send()


def shards(
    attn_inputs,
    queries,
    key_vectors,
    logp_grad,
    new_logp,
    old_logp,
    rewards,
    group_ids,
    lengths,
    value_proj,
    first_moment,
    second_moment,
):
    vmem = pl.BlockSpec(memory_space=pltpu.VMEM)
    hbm = pl.BlockSpec(memory_space=pl.ANY)
    dma = pltpu.SemaphoreType.DMA
    bf, f32, i32 = jnp.bfloat16, jnp.float32, jnp.int32

    def buf(*shape, kind=bf):
        return pltpu.VMEM(shape, kind)

    return pl.pallas_call(
        kernel,
        out_shape=(
            jax.ShapeDtypeStruct((128, 5120), bf),
            jax.ShapeDtypeStruct((160, 512), bf),
            jax.ShapeDtypeStruct((10, 512), bf),
            jax.ShapeDtypeStruct((10, 512), bf),
        ),
        in_specs=[hbm] * 10 + [vmem] * 2,
        out_specs=(vmem,) * 4,
        scratch_shapes=[
            buf(128, 2560),
            buf(128, 2560),
            buf(128, 512),
            buf(128, 5120),
            buf(160, 512),
            buf(1, 128, kind=f32),
            buf(1, 128, kind=f32),
            buf(1, 32, kind=f32),
            buf(1, 32, kind=i32),
            buf(1, 32, kind=i32),
            buf(NZ, 2, 64, 512),
            buf(128, 2560),
            buf(64, 2560),
            buf(64, 2560),
            buf(KVH, QB, HEAD),
            buf(KVH, QB, HEAD),
            buf(8, KVH, 256, QB),
            buf(8, KVH, 1, QB, kind=f32),
            buf(KVH, 1, QB, kind=f32),
            buf(KVH, 1, QB, kind=f32),
            buf(2, 128, 512, kind=f32),
            buf(2, 8, 2, 64, 512),
            buf(2, 8, 2, 64, 512),
            buf(64, 512),
            buf(64, 512),
            buf(8, 4, 160, 128),
            buf(4, 160, 1024),
            buf(32, 160, 512),
            buf(32, 512),
            buf(16, 32, 512),
            buf(160, 512, kind=f32),
            buf(160, 512, kind=f32),
            buf(8, 128, 512),
            buf(640, 512, kind=f32),
            buf(3, 640, 128),
            buf(3, 640, 128),
            buf(4, 160, 128, kind=f32),
            buf(4, 160, 128),
            buf(NZ, 160, 128),
            buf(160, 128),
            buf(4, 160, 128),
            dma((10,)),
            dma((5,)),
            dma((5,)),
            dma((2, 8, 2)),
            dma((2, 8, 2)),
            dma((2, 8, 2)),
            dma((2, 8, 2)),
            dma((8,)),
            dma((8,)),
            dma((2, 8)),
            dma((2, 8)),
            dma((4,)),
            dma((4,)),
            dma((16,)),
            dma((16,)),
            dma((8,)),
            dma((8,)),
            dma((3,)),
            dma((3,)),
            dma((4,)),
            dma((16,)),
            dma((3,)),
            dma,
            dma((4,)),
            dma((4,)),
        ],
        compiler_params=pltpu.CompilerParams(
            collective_id=0, has_side_effects=True, vmem_limit_bytes=60 * 1024 * 1024
        ),
    )(
        attn_inputs,
        queries,
        key_vectors,
        logp_grad,
        new_logp.reshape(1, 128),
        old_logp.reshape(1, 128),
        rewards.reshape(1, 32),
        group_ids.reshape(1, 32),
        lengths.reshape(1, 32),
        value_proj,
        first_moment,
        second_moment,
    )


def solution(mesh):
    torus = Mesh(mesh.devices.reshape(2, 16, 4, 2, 2), AXES)
    placed = (
        P(SIDE_FSDP, None),
        P(SIDE_FSDP, None),
        P(SIDE_FSDP, None),
        P(SIDE_FSDP, None),
        P(SIDE_FSDP),
        P(SIDE_FSDP),
        P(),
        P(),
        P(),
        P(FSDP, None),
        P(FSDP_SIDE, None),
        P(FSDP_SIDE, None),
    )
    return jax.shard_map(
        shards,
        mesh=torus,
        in_specs=placed,
        out_specs=(P(SIDE_FSDP, None), P(FSDP, None), P(FSDP_SIDE, None), P(FSDP_SIDE, None)),
        check_vma=False,
    )
```

```python
import math

import jax
import jax.numpy as jnp
from jax import lax
from jax.experimental import pallas as pl
from jax.experimental.pallas import tpu as pltpu
from jax.sharding import Mesh
from jax.sharding import PartitionSpec as P

AXES = ("xl", "z", "y", "xh", "core")
FSDP = ("xl", "z")
SIDE = ("y", "xh", "core")
SIDE_FSDP = SIDE + FSDP
FSDP_SIDE = FSDP + SIDE
MESH = pl.DeviceIdType.MESH
NZ = 16
KVH = 4
PER = 5
HEAD = 128
QB = PER * 128
EXP_SCALE = math.log2(math.e) / math.sqrt(HEAD)
LOW = -1e30

clip_low = 0.8
clip_high = 1.2
decay_first = 0.9
decay_second = 0.95
step_rate = 0.001
weight_decay = 0.1
adam_eps = 1e-08
bias_first = 1.0 - 0.9**10
bias_second = 1.0 - 0.95**10


def coefficient_row(new_ref, old_ref, rew_ref, gid_ref, len_ref, side, first_pos):
    rew = rew_ref[...]
    gid = gid_ref[...]
    lens = len_ref[...]
    roll_of = lax.broadcasted_iota(jnp.int32, rew.shape, 1)
    adv_parts, len_parts = [], []
    for roll in range(2):
        own = roll_of == side * 2 + roll
        own_gid = jnp.sum(jnp.where(own, gid, 0), axis=1, keepdims=True)
        own_rew = jnp.sum(jnp.where(own, rew, 0.0), axis=1, keepdims=True)
        own_len = jnp.sum(jnp.where(own, lens, 0), axis=1, keepdims=True)
        member = jnp.where(gid == own_gid, 1.0, 0.0)
        count = jnp.maximum(jnp.sum(member, axis=1, keepdims=True), 1.0)
        mean = jnp.sum(member * rew, axis=1, keepdims=True) / count
        spread = rew - mean
        var = jnp.sum(member * (spread * spread), axis=1, keepdims=True) / count
        adv_parts.append((own_rew - mean) / jnp.maximum(jnp.sqrt(var), 1.0))
        len_parts.append(own_len)
    slot = lax.broadcasted_iota(jnp.int32, (1, 128), 1)
    first = slot < 64
    adv = jnp.where(first, adv_parts[0], adv_parts[1])
    length = jnp.where(first, len_parts[0], len_parts[1])
    pos = first_pos + jnp.where(first, slot, slot - 64)
    ratio = jnp.exp(new_ref[...] - old_ref[...])
    clipped = jnp.minimum(jnp.maximum(ratio, clip_low), clip_high)
    active = (ratio * adv <= clipped * adv) & (pos < length)
    return jnp.where(active, -adv * ratio * (2048.0 / length.astype(jnp.float32)), 0.0)


def adam_rows(weight_now, grad_rows, first_moment, second_moment):
    first = decay_first * first_moment + (1.0 - decay_first) * grad_rows
    second = decay_second * second_moment + (1.0 - decay_second) * grad_rows * grad_rows
    update = (
        first / bias_first / (jnp.sqrt(second / bias_second) + adam_eps) + weight_decay * weight_now
    )
    return weight_now - step_rate * update, first, second


def kernel(
    x_hbm,
    q_hbm,
    k_hbm,
    g_hbm,
    new_hbm,
    old_hbm,
    rew_hbm,
    gid_hbm,
    len_hbm,
    w_hbm,
    m1_ref,
    m2_ref,
    ig_ref,
    np_ref,
    nf_ref,
    ns_ref,
    qv,
    gv,
    kv,
    xv,
    wv,
    newv,
    oldv,
    rewv,
    gidv,
    lenv,
    kbuf,
    gsend,
    qst,
    gst,
    qh,
    gh,
    eb,
    mst,
    mrow,
    lrow,
    pbuf,
    pown,
    rsend,
    rrecv,
    vsend,
    vrecv,
    xt,
    xg,
    wfull,
    mv,
    moms,
    m1f,
    m2f,
    vga,
    acc,
    xs,
    xr,
    zsum,
    zs,
    zr,
    gy,
    gf,
    load_sem,
    x_send,
    x_recv,
    ag_send,
    ag_recv,
    rs_send,
    rs_recv,
    in_send,
    in_recv,
    wz_send,
    wz_recv,
    wy_send,
    wy_recv,
    mo_send,
    mo_recv,
    va_send,
    va_recv,
    xs_send,
    xs_recv,
    zs_send,
    zs_recv,
    gy_send,
    gy_recv,
    gf_send,
    gf_recv,
    known,
):
    xl = lax.axis_index("xl")
    z = lax.axis_index("z")
    y = lax.axis_index("y")
    xh = lax.axis_index("xh")
    core = lax.axis_index("core")
    side = (y * 2 + xh) * 2 + core
    x = xh * 2 + xl
    up = lax.rem(z + 1, NZ)
    down = lax.rem(z + NZ - 1, NZ)
    mine = pl.ds(pl.multiple_of(64 * xl, 64), 64)
    theirs = pl.ds(pl.multiple_of(64 * (1 - xl), 64), 64)

    def lanes(index):
        return pl.ds(pl.multiple_of(index * 128, 128), 128)

    def y_at(step):
        return lax.rem(y + step, 4)

    loads = [
        pltpu.make_async_copy(src, dst, load_sem.at[i])
        for i, (src, dst) in enumerate(
            (
                (k_hbm, kv),
                (q_hbm, qv),
                (w_hbm, wv),
                (new_hbm, newv),
                (old_hbm, oldv),
                (rew_hbm, rewv),
                (gid_hbm, gidv),
                (len_hbm, lenv),
                (g_hbm, gv),
                (x_hbm, xv),
            )
        )
    ]
    for load in loads:
        load.start()

    barrier = pltpu.get_barrier_semaphore()

    def greet(**where):
        pl.semaphore_signal(barrier, inc=1, device_id=where, device_id_type=MESH)

    beside = [{"xl": 1 - xl, "xh": xh}, {"xl": 1 - xl, "xh": 1 - xh}]
    around = [{"y": y_at(1)}, {"y": y_at(3)}]
    greet(z=up)
    greet(z=down)
    greet(**beside[0])
    greet(core=1 - core)
    for where in around + beside[1:]:
        greet(**where)

    def hello(kind, to):
        for where in to:
            pl.semaphore_signal(known.at[kind], inc=1, device_id=where, device_id_type=MESH)

    def heard(kind, to):
        pl.semaphore_wait(known.at[kind], len(to))

    mv[...] = jnp.zeros(mv.shape, mv.dtype)
    mv[0:10, :] = m1_ref[...]
    mv[16:26, :] = m2_ref[...]
    moms[side] = mv[...]
    loads[0].wait()
    kbuf[z, pl.ds(2 * xl, 2)] = kv[mine, :].reshape(2, 32, 512)
    for i in range(1, 3):
        loads[i].wait()
    pl.semaphore_wait(barrier, 7)

    def copy_to(src, dst, send, recv, **where):
        return pltpu.make_async_remote_copy(
            src_ref=src,
            dst_ref=dst,
            send_sem=send,
            recv_sem=recv,
            device_id=where,
            device_id_type=MESH,
        )

    def pair_copy(src, dst, at):
        return copy_to(src, dst, x_send.at[at], x_recv.at[at], xl=1 - xl)

    def ring_block(way, step):
        back = step - 1
        return lax.rem(z + NZ - back, NZ) if way == 0 else lax.rem(z + back, NZ)

    def key_copy(way, step, piece):
        part = kbuf.at[ring_block(way, step), piece]
        return copy_to(
            part,
            part,
            ag_send.at[way, step - 1, piece],
            ag_recv.at[way, step - 1, piece],
            z=up if way == 0 else down,
        )

    def weight_copy(way, step):
        part = wfull.at[core * NZ + ring_block(way, step), :, lanes(y)]
        return copy_to(
            part,
            part,
            wz_send.at[way, step - 1],
            wz_recv.at[way, step - 1],
            z=up if way == 0 else down,
        )

    def part_copy(way, step, piece):
        return copy_to(
            rsend.at[way, step, piece],
            rrecv.at[way, step, piece],
            rs_send.at[way, step, piece],
            rs_recv.at[way, step, piece],
            z=up if way == 0 else down,
        )

    def key_pair(i):
        rows = pl.ds(pl.multiple_of(64 * (1 - xl) + 32 * i, 32), 32)
        return pair_copy(kv.at[rows], kbuf.at[z, 2 * xl + i], 5 * i)

    query_pair = pair_copy(qv.at[theirs], qst, 1)
    grad_pair = pair_copy(gsend.at[theirs], gst, 2)
    own_weight = wfull.at[core * NZ + z, :, lanes(y)]
    weight_pair = pair_copy(wv.at[:, lanes(y)], own_weight, 3)
    for i in range(2):
        key_pair(i).start()
        for way in range(2):
            key_copy(way, 1, 2 * xl + i).start()

    @pl.when(core == xl)
    def _():
        weight_pair.start()
        wfull[core * NZ + z, :, lanes(y)] = wv[:, lanes(y)]

    query_pair.start()
    hello(0, around + beside[:1] + [{"core": 1 - core}])
    for i in range(2):
        key_pair(i).wait_recv()
        for way in range(2):
            key_copy(way, 1, 2 * (1 - xl) + i).start()

    for i in range(3, 9):
        loads[i].wait()
    coeff = coefficient_row(newv, oldv, rewv, gidv, lenv, side, (xl * NZ + z) * 64)
    diag = lax.broadcasted_iota(jnp.int32, (128, 128), 0) == lax.broadcasted_iota(
        jnp.int32, (128, 128), 1
    )
    coeff_col = jnp.sum(jnp.where(diag, coeff, 0.0), axis=1, keepdims=True)
    for head in range(KVH * PER):
        cols = slice(head * HEAD, (head + 1) * HEAD)
        gsend[:, cols] = (coeff_col * gv[:, cols].astype(jnp.float32)).astype(jnp.bfloat16)
    grad_pair.start()


    @pl.when(core != xl)
    def _():
        weight_pair.wait_recv()

    for way in range(2):
        weight_copy(way, 1).start()

    def spread(dst, src, rows, half):
        for head in range(KVH * PER):
            at = pl.ds(pl.multiple_of(64 * half, 64) + (head % PER) * 128, 64)
            dst[head // PER, at, :] = src[rows, head * HEAD : (head + 1) * HEAD]

    spread(qh, qv, mine, xl)
    spread(gh, gsend, mine, xl)
    mrow[...] = jnp.full(mrow.shape, LOW, jnp.float32)
    lrow[...] = jnp.zeros(lrow.shape, jnp.float32)

    def arrived(step):
        for i in range(4):
            piece = lax.rem(2 * xl + i, 4)
            for way in range(2):
                if way == 1 and step == 8:
                    continue
                key_copy(way, step, piece).wait_recv()
                if step < 8 - way:
                    key_copy(way, step + 1, piece).start()
        for way in range(2 * (step < 8) + (step == 8)):
            weight_copy(way, step).wait_recv()
            if step < 8 - way:
                weight_copy(way, step + 1).start()

    loads[9].wait()

    def turn(n, carry):
        cols = pl.ds(pl.multiple_of(n * 640, 128), 640)
        xt[n] = xv[:, cols].T.reshape(4, 160, 128)
        return carry

    def input_copies():
        copies = []
        for step in range(4):
            for flip in range(2):
                if step + flip:
                    there = core ^ flip
                    copies.append(
                        copy_to(
                            xt.at[pl.ds(4 * there, 4), y_at(step)],
                            xg.at[:, :, lanes(2 * y + core)],
                            in_send.at[step * 2 + flip],
                            in_recv.at[step * 2 + flip],
                            y=y_at(step),
                            core=there,
                        )
                    )
        return copies

    def moment_copies():
        copies = []
        for step in range(4):
            for flip in range(4):
                if step + flip:
                    copies.append(
                        copy_to(
                            mv,
                            moms.at[side],
                            mo_send.at[step * 4 + flip],
                            mo_recv.at[step * 4 + flip],
                            y=y_at(step),
                            xh=xh ^ (flip & 1),
                            core=core ^ (flip >> 1),
                        )
                    )
        return copies

    row = lax.broadcasted_iota(jnp.int32, (256, 1), 0)
    lane = lax.broadcasted_iota(jnp.int32, (1, QB), 1)
    in_head = lax.rem(lane, 128)
    qpos = jnp.where(in_head < 64, in_head, in_head - 64 + 1024) + z * 64
    in_block = lax.rem(row, 128)
    kpos_base = jnp.where(in_block < 64, in_block, in_block - 64 + 1024)

    def score(index, carry):
        t = index // KVH + 1
        head = lax.rem(index, KVH)
        a = lax.rem(z + NZ - t, NZ)
        b = lax.rem(z + jnp.where(t == 8, 0, t), NZ)
        keys = jnp.concatenate(
            [
                kbuf[a, :, :, lanes(head)].reshape(128, HEAD),
                kbuf[b, :, :, lanes(head)].reshape(128, HEAD),
            ],
            axis=0,
        )
        s = lax.dot_general(
            keys, qh[head], (((1,), (1,)), ((), ())), preferred_element_type=jnp.float32
        )
        kpos = kpos_base + jnp.where(row < 128, a, b) * 64
        s = jnp.where(kpos <= qpos, s, LOW)
        old = mrow[head]
        top = jnp.maximum(old, jnp.max(s, axis=0, keepdims=True))
        e = jnp.exp2((s - top) * EXP_SCALE)
        lrow[head] = lrow[head] * jnp.exp2((old - top) * EXP_SCALE) + jnp.sum(
            e, axis=0, keepdims=True
        )
        mrow[head] = top
        mst[t - 1, head] = top
        eb[t - 1, head] = e.astype(jnp.bfloat16)
        return carry

    def scores(first, last):
        lax.fori_loop((first - 1) * KVH, last * KVH, score, 0)

    arrived(1)
    heard(0, range(4))
    hello(1, [{"core": 1 - core}])
    lax.fori_loop(0, 4, turn, 0)
    arrived(2)
    heard(1, range(1))
    hello(2, beside)
    lax.fori_loop(4, 8, turn, 0)
    xg[:, :, lanes(2 * y + core)] = xt[pl.ds(4 * core, 4), y]
    for copy in input_copies():
        copy.start()
    arrived(3)
    heard(2, range(2))
    hello(3, beside)
    query_pair.wait_recv()
    spread(qh, qst, slice(None), 1 - xl)
    arrived(4)
    heard(3, range(2))
    for copy in moment_copies():
        copy.start()
    scores(1, 2)
    arrived(5)
    scores(3, 4)
    arrived(6)
    scores(5, 5)
    arrived(7)
    scores(6, 7)
    grad_pair.wait_recv()
    spread(gh, gst, slice(None), 1 - xl)
    arrived(8)

    def across_y(step):
        part = wfull.at[pl.ds(NZ * core, NZ), :, lanes(y)]
        return copy_to(part, part, wy_send.at[step], wy_recv.at[step], y=y_at(step))

    def across_core():
        part = wfull.at[pl.ds(NZ * core, NZ)]
        return copy_to(part, part, wy_send.at[0], wy_recv.at[0], core=1 - core)

    for step in range(1, 4):
        across_y(step).start()
    scores(8, 8)

    lrow[...] = 1.0 / lrow[...]

    def parts(t, dst):
        for head in range(KVH):
            scale = jnp.exp2((mst[t - 1, head] - mrow[head]) * EXP_SCALE) * lrow[head]
            p = (eb[t - 1, head].astype(jnp.float32) * scale).astype(jnp.bfloat16)
            dst[:, head * HEAD : (head + 1) * HEAD] = jnp.dot(
                p, gh[head], preferred_element_type=jnp.float32
            )

    def pass_on(way, step, src, piece, first):
        value = src[piece * 32 : (piece + 1) * 32, :]
        if not first:
            part_copy(way, step - 1, piece).wait_recv()
            value = value + rrecv[way, step - 1, piece].astype(jnp.float32)
        rsend[way, step, piece] = value.astype(jnp.bfloat16)
        part_copy(way, step, piece).start()

    parts(8, pbuf.at[0])
    for piece in range(4):
        pass_on(0, 0, pbuf.at[0, pl.ds(0, 128)], piece, True)
    pown[...] = pbuf[0, 128:256, :]
    parts(7, pbuf.at[1])
    for piece in range(4):
        pass_on(1, 0, pbuf.at[1, pl.ds(0, 128)], piece, True)
    for piece in range(4):
        pass_on(0, 1, pbuf.at[1, pl.ds(128, 128)], piece, False)

    def ring_step(i, carry):
        now = pbuf.at[lax.rem(i, 2)]
        parts(8 - i, now)
        for piece in range(4):
            pass_on(1, i - 1, now.at[pl.ds(0, 128)], piece, False)
            pass_on(0, i, now.at[pl.ds(128, 128)], piece, False)
        return carry

    lax.fori_loop(2, 8, ring_step, 0)

    for copy in moment_copies():
        copy.wait_recv()
    for s in range(16):
        m1f[10 * s : 10 * s + 10, :] = moms[s, 0:10, :].astype(jnp.float32)
        m2f[10 * s : 10 * s + 10, :] = moms[s, 16:26, :].astype(jnp.float32)

    value_pair = pair_copy(vsend, vrecv, 4)
    for piece in range(4):
        part_copy(1, 6, piece).wait_recv()
        part_copy(0, 7, piece).wait_recv()

    def block_rows(half):
        rows = pl.ds(2 * half, 2)
        return (
            pown[pl.ds(pl.multiple_of(64 * half, 64), 64), :]
            + rrecv[1, 6, rows].reshape(64, 512).astype(jnp.float32)
            + rrecv[0, 7, rows].reshape(64, 512).astype(jnp.float32)
        ).astype(jnp.bfloat16)

    vsend[...] = block_rows(1 - xl)
    value_pair.start()
    slot = 2 * y + core
    vga[slot, mine, :] = block_rows(xl)
    value_pair.wait_recv()
    vga[slot, theirs, :] = vrecv[...]

    def values_y(step):
        return copy_to(vga.at[slot], vga.at[slot], va_send.at[step], va_recv.at[step], y=y_at(step))

    def values_core(step):
        part = vga.at[2 * lax.rem(y + 4 - step, 4) + core]
        return copy_to(part, part, va_send.at[4 + step], va_recv.at[4 + step], core=1 - core)

    for step in (2, 1, 3):
        values_y(step).start()
    values_core(0).start()

    for copy in input_copies():
        copy.wait_recv()
    for step in range(1, 4):
        across_y(step).wait_recv()
    across_core().start()

    def add_inputs(step, first):
        at = lax.rem(y + 4 - step, 4)
        a = xg[:, :, pl.ds(pl.multiple_of(at * 256, 256), 256)].reshape(640, 256)
        b = vga[pl.ds(2 * at, 2)].reshape(256, 512)
        value = jnp.dot(a, b, preferred_element_type=jnp.float32)
        acc[...] = value if first else acc[...] + value

    values_core(0).wait_recv()
    add_inputs(0, True)
    for step in (1, 3, 2):
        values_y(step).wait_recv()
        values_core(step).start()
        values_core(step).wait_recv()
        add_inputs(step, False)

    def sum_x(step):
        at = lax.rem(x + step, 4)
        return copy_to(
            xs.at[step - 1],
            xr.at[step - 1],
            xs_send.at[step - 1],
            xs_recv.at[step - 1],
            xl=lax.rem(at, 2),
            xh=at // 2,
        )

    for step in (2, 1, 3):
        at = lax.rem(x + step, 4)
        xs[step - 1] = acc[:, lanes(at)].astype(jnp.bfloat16)
        sum_x(step).start()

    across_core().wait_recv()

    def grad_tile(n, carry):
        w = wfull[pl.ds(4 * n, 4)].reshape(640, 512)
        ig_ref[:, pl.ds(pl.multiple_of(n * 640, 128), 640)] = lax.dot_general(
            vga[slot], w, (((1,), (1,)), ((), ())), preferred_element_type=jnp.float32
        ).astype(jnp.bfloat16)
        return carry

    lax.fori_loop(0, 8, grad_tile, 0)

    for step in (1, 3, 2):
        sum_x(step).wait_recv()
    total = acc[:, lanes(x)]
    for step in range(3):
        total = total + xr[step].astype(jnp.float32)
    zsum[...] = total.reshape(4, 160, 128)
    zs[...] = zsum[...].astype(jnp.bfloat16)

    def sum_z(j):
        at = 4 * j + y
        far = lax.rem(z - at + NZ, NZ)
        return copy_to(zs.at[j], zr.at[far], zs_send.at[j], zs_recv.at[far], z=at)

    for j in range(4):

        @pl.when(z != 4 * j + y)
        def _(j=j):
            sum_z(j).start()

    root = lax.rem(z, 4) == y

    def spread_y(step):
        return copy_to(gy, gy, gy_send.at[step - 1], gy_recv, y=y_at(step))

    @pl.when(root)
    def _():
        total = zsum[z // 4]
        for far in range(1, NZ):
            copy_to(zs.at[0], zr.at[far], zs_send.at[0], zs_recv.at[far], z=up).wait_recv()
            total = total + zr[far].astype(jnp.float32)
        gy[...] = total.astype(jnp.bfloat16)
        for step in range(1, 4):
            spread_y(step).start()

    @pl.when(jnp.logical_not(root))
    def _():
        spread_y(1).wait_recv()

    def spread_x(to_xh, to_core):
        k = to_xh * 2 + to_core
        return copy_to(
            gy, gf.at[x], gf_send.at[k], gf_recv.at[x], xl=core, xh=to_xh, core=to_core
        )

    def is_self(to_xh, to_core):
        return (xl == core) & (xh == to_xh) & (core == to_core)

    for to_xh in range(2):
        for to_core in range(2):

            @pl.when(jnp.logical_not(is_self(to_xh, to_core)))
            def _(to_xh=to_xh, to_core=to_core):
                spread_x(to_xh, to_core).start()

    @pl.when(xl == core)
    def _():
        gf[x] = gy[...]

    for at in range(4):

        @pl.when(jnp.logical_not((xl == core) & (x == at)))
        def _(at=at):
            copy_to(gy, gf.at[at], gf_send.at[0], gf_recv.at[at], core=1 - core).wait_recv()

    for at in range(4):
        cols = slice(at * 128, (at + 1) * 128)
        new, first, second = adam_rows(
            wv[:, cols].astype(jnp.float32),
            gf[at].astype(jnp.float32),
            m1f[:, cols],
            m2f[:, cols],
        )
        np_ref[:, cols] = new.astype(jnp.bfloat16)
        m1f[:, cols] = first
        m2f[:, cols] = second
    for s in range(16):

        @pl.when(side == s)
        def _(s=s):
            nf_ref[...] = m1f[10 * s : 10 * s + 10, :].astype(jnp.bfloat16)
            ns_ref[...] = m2f[10 * s : 10 * s + 10, :].astype(jnp.bfloat16)

    for way in range(2):
        for step in range(8 - way):
            weight_copy(way, step + 1).wait_send()
            for piece in range(4):
                key_copy(way, step + 1, piece).wait_send()
                part_copy(way, step, piece).wait_send()
    for copy in (key_pair(0), key_pair(1), query_pair, grad_pair, value_pair):
        copy.wait_send()

    @pl.when(core == xl)
    def _():
        weight_pair.wait_send()

    for copy in input_copies() + moment_copies():
        copy.wait_send()
    across_core().wait_send()
    values_core(0).wait_send()
    for step in range(1, 4):
        across_y(step).wait_send()
        values_y(step).wait_send()
        values_core(step).wait_send()
        sum_x(step).wait_send()
    for j in range(4):

        @pl.when(z != 4 * j + y)
        def _(j=j):
            sum_z(j).wait_send()

    @pl.when(root)
    def _():
        for step in range(1, 4):
            spread_y(step).wait_send()

    for to_xh in range(2):
        for to_core in range(2):

            @pl.when(jnp.logical_not(is_self(to_xh, to_core)))
            def _(to_xh=to_xh, to_core=to_core):
                spread_x(to_xh, to_core).wait_send()


def shards(
    attn_inputs,
    queries,
    key_vectors,
    logp_grad,
    new_logp,
    old_logp,
    rewards,
    group_ids,
    lengths,
    value_proj,
    first_moment,
    second_moment,
):
    vmem = pl.BlockSpec(memory_space=pltpu.VMEM)
    hbm = pl.BlockSpec(memory_space=pl.ANY)
    dma = pltpu.SemaphoreType.DMA
    bf, f32, i32 = jnp.bfloat16, jnp.float32, jnp.int32

    def buf(*shape, kind=bf):
        return pltpu.VMEM(shape, kind)

    return pl.pallas_call(
        kernel,
        out_shape=(
            jax.ShapeDtypeStruct((128, 5120), bf),
            jax.ShapeDtypeStruct((160, 512), bf),
            jax.ShapeDtypeStruct((10, 512), bf),
            jax.ShapeDtypeStruct((10, 512), bf),
        ),
        in_specs=[hbm] * 10 + [vmem] * 2,
        out_specs=(vmem,) * 4,
        scratch_shapes=[
            buf(128, 2560),
            buf(128, 2560),
            buf(128, 512),
            buf(128, 5120),
            buf(160, 512),
            buf(1, 128, kind=f32),
            buf(1, 128, kind=f32),
            buf(1, 32, kind=f32),
            buf(1, 32, kind=i32),
            buf(1, 32, kind=i32),
            buf(NZ, 4, 32, 512),
            buf(128, 2560),
            buf(64, 2560),
            buf(64, 2560),
            buf(KVH, QB, HEAD),
            buf(KVH, QB, HEAD),
            buf(8, KVH, 256, QB),
            buf(8, KVH, 1, QB, kind=f32),
            buf(KVH, 1, QB, kind=f32),
            buf(KVH, 1, QB, kind=f32),
            buf(2, 256, 512, kind=f32),
            buf(128, 512, kind=f32),
            buf(2, 8, 4, 32, 512),
            buf(2, 8, 4, 32, 512),
            buf(64, 512),
            buf(64, 512),
            buf(8, 4, 160, 128),
            buf(4, 160, 1024),
            buf(32, 160, 512),
            buf(32, 512),
            buf(16, 32, 512),
            buf(160, 512, kind=f32),
            buf(160, 512, kind=f32),
            buf(8, 128, 512),
            buf(640, 512, kind=f32),
            buf(3, 640, 128),
            buf(3, 640, 128),
            buf(4, 160, 128, kind=f32),
            buf(4, 160, 128),
            buf(NZ, 160, 128),
            buf(160, 128),
            buf(4, 160, 128),
            dma((10,)),
            dma((6,)),
            dma((6,)),
            dma((2, 8, 4)),
            dma((2, 8, 4)),
            dma((2, 8, 4)),
            dma((2, 8, 4)),
            dma((8,)),
            dma((8,)),
            dma((2, 8)),
            dma((2, 8)),
            dma((4,)),
            dma((4,)),
            dma((16,)),
            dma((16,)),
            dma((8,)),
            dma((8,)),
            dma((3,)),
            dma((3,)),
            dma((4,)),
            dma((16,)),
            dma((3,)),
            dma,
            dma((4,)),
            dma((4,)),
            pltpu.SemaphoreType.REGULAR((4,)),
        ],
        compiler_params=pltpu.CompilerParams(
            collective_id=0, has_side_effects=True, vmem_limit_bytes=60 * 1024 * 1024
        ),
    )(
        attn_inputs,
        queries,
        key_vectors,
        logp_grad,
        new_logp.reshape(1, 128),
        old_logp.reshape(1, 128),
        rewards.reshape(1, 32),
        group_ids.reshape(1, 32),
        lengths.reshape(1, 32),
        value_proj,
        first_moment,
        second_moment,
    )


def solution(mesh):
    torus = Mesh(mesh.devices.reshape(2, 16, 4, 2, 2), AXES)
    placed = (
        P(SIDE_FSDP, None),
        P(SIDE_FSDP, None),
        P(SIDE_FSDP, None),
        P(SIDE_FSDP, None),
        P(SIDE_FSDP),
        P(SIDE_FSDP),
        P(),
        P(),
        P(),
        P(FSDP, None),
        P(FSDP_SIDE, None),
        P(FSDP_SIDE, None),
    )
    return jax.shard_map(
        shards,
        mesh=torus,
        in_specs=placed,
        out_specs=(P(SIDE_FSDP, None), P(FSDP, None), P(FSDP_SIDE, None), P(FSDP_SIDE, None)),
        check_vma=False,
    )
```

```python
import math

import jax
import jax.numpy as jnp
from jax import lax
from jax.experimental import pallas as pl
from jax.experimental.pallas import tpu as pltpu
from jax.sharding import Mesh
from jax.sharding import PartitionSpec as P

AXES = ("xl", "z", "y", "xh", "core")
FSDP = ("xl", "z")
SIDE = ("y", "xh", "core")
SIDE_FSDP = SIDE + FSDP
FSDP_SIDE = FSDP + SIDE
MESH = pl.DeviceIdType.MESH
NZ = 16
KVH = 4
PER = 5
HEAD = 128
QB = PER * 128
EXP_SCALE = math.log2(math.e) / math.sqrt(HEAD)
LOW = -1e30

clip_low = 0.8
clip_high = 1.2
decay_first = 0.9
decay_second = 0.95
step_rate = 0.001
weight_decay = 0.1
adam_eps = 1e-08
bias_first = 1.0 - 0.9**10
bias_second = 1.0 - 0.95**10


def coefficient_row(new_ref, old_ref, rew_ref, gid_ref, len_ref, side, first_pos):
    rew = rew_ref[...]
    gid = gid_ref[...]
    lens = len_ref[...]
    roll_of = lax.broadcasted_iota(jnp.int32, rew.shape, 1)
    adv_parts, len_parts = [], []
    for roll in range(2):
        own = roll_of == side * 2 + roll
        own_gid = jnp.sum(jnp.where(own, gid, 0), axis=1, keepdims=True)
        own_rew = jnp.sum(jnp.where(own, rew, 0.0), axis=1, keepdims=True)
        own_len = jnp.sum(jnp.where(own, lens, 0), axis=1, keepdims=True)
        member = jnp.where(gid == own_gid, 1.0, 0.0)
        count = jnp.maximum(jnp.sum(member, axis=1, keepdims=True), 1.0)
        mean = jnp.sum(member * rew, axis=1, keepdims=True) / count
        spread = rew - mean
        var = jnp.sum(member * (spread * spread), axis=1, keepdims=True) / count
        adv_parts.append((own_rew - mean) / jnp.maximum(jnp.sqrt(var), 1.0))
        len_parts.append(own_len)
    slot = lax.broadcasted_iota(jnp.int32, (1, 128), 1)
    first = slot < 64
    adv = jnp.where(first, adv_parts[0], adv_parts[1])
    length = jnp.where(first, len_parts[0], len_parts[1])
    pos = first_pos + jnp.where(first, slot, slot - 64)
    ratio = jnp.exp(new_ref[...] - old_ref[...])
    clipped = jnp.minimum(jnp.maximum(ratio, clip_low), clip_high)
    active = (ratio * adv <= clipped * adv) & (pos < length)
    return jnp.where(active, -adv * ratio * (2048.0 / length.astype(jnp.float32)), 0.0)


def adam_rows(weight_now, grad_rows, first_moment, second_moment):
    first = decay_first * first_moment + (1.0 - decay_first) * grad_rows
    second = decay_second * second_moment + (1.0 - decay_second) * grad_rows * grad_rows
    update = (
        first / bias_first / (jnp.sqrt(second / bias_second) + adam_eps) + weight_decay * weight_now
    )
    return weight_now - step_rate * update, first, second


def kernel(
    x_hbm,
    q_hbm,
    k_hbm,
    g_hbm,
    new_hbm,
    old_hbm,
    rew_hbm,
    gid_hbm,
    len_hbm,
    w_hbm,
    m1_ref,
    m2_ref,
    ig_ref,
    np_ref,
    nf_ref,
    ns_ref,
    qv,
    gv,
    kv,
    xv,
    wv,
    newv,
    oldv,
    rewv,
    gidv,
    lenv,
    kbuf,
    gsend,
    qst,
    gst,
    qh,
    gh,
    eb,
    mst,
    mrow,
    lrow,
    pbuf,
    pown,
    rsend,
    rrecv,
    vsend,
    vrecv,
    xt,
    xg,
    wfull,
    mv,
    moms,
    m1f,
    m2f,
    vga,
    acc,
    xs,
    xr,
    zsum,
    zs,
    zr,
    gy,
    gf,
    load_sem,
    x_send,
    x_recv,
    ag_send,
    ag_recv,
    rs_send,
    rs_recv,
    in_send,
    in_recv,
    wz_send,
    wz_recv,
    wy_send,
    wy_recv,
    mo_send,
    mo_recv,
    va_send,
    va_recv,
    xs_send,
    xs_recv,
    zs_send,
    zs_recv,
    gy_send,
    gy_recv,
    gf_send,
    gf_recv,
    known,
):
    xl = lax.axis_index("xl")
    z = lax.axis_index("z")
    y = lax.axis_index("y")
    xh = lax.axis_index("xh")
    core = lax.axis_index("core")
    side = (y * 2 + xh) * 2 + core
    x = xh * 2 + xl
    up = lax.rem(z + 1, NZ)
    down = lax.rem(z + NZ - 1, NZ)
    mine = pl.ds(pl.multiple_of(64 * xl, 64), 64)
    theirs = pl.ds(pl.multiple_of(64 * (1 - xl), 64), 64)

    def lanes(index):
        return pl.ds(pl.multiple_of(index * 128, 128), 128)

    def y_at(step):
        return lax.rem(y + step, 4)

    loads = [
        pltpu.make_async_copy(src, dst, load_sem.at[i])
        for i, (src, dst) in enumerate(
            (
                (k_hbm, kv),
                (q_hbm, qv),
                (w_hbm, wv),
                (new_hbm, newv),
                (old_hbm, oldv),
                (rew_hbm, rewv),
                (gid_hbm, gidv),
                (len_hbm, lenv),
                (g_hbm, gv),
                (x_hbm, xv),
            )
        )
    ]
    for load in loads:
        load.start()

    barrier = pltpu.get_barrier_semaphore()

    def greet(**where):
        pl.semaphore_signal(barrier, inc=1, device_id=where, device_id_type=MESH)

    beside = [{"xl": 1 - xl, "xh": xh}, {"xl": 1 - xl, "xh": 1 - xh}]
    around = [{"y": y_at(1)}, {"y": y_at(3)}]
    greet(z=up)
    greet(z=down)
    greet(**beside[0])
    greet(core=1 - core)
    for where in around + beside[1:]:
        greet(**where)

    def hello(kind, to):
        for where in to:
            pl.semaphore_signal(known.at[kind], inc=1, device_id=where, device_id_type=MESH)

    def heard(kind, to):
        pl.semaphore_wait(known.at[kind], len(to))

    mv[...] = jnp.zeros(mv.shape, mv.dtype)
    mv[0:10, :] = m1_ref[...]
    mv[16:26, :] = m2_ref[...]
    moms[side] = mv[...]
    loads[0].wait()
    kbuf[z, pl.ds(2 * xl, 2)] = kv[mine, :].reshape(2, 32, 512)
    for i in range(1, 3):
        loads[i].wait()
    pl.semaphore_wait(barrier, 7)

    def copy_to(src, dst, send, recv, **where):
        return pltpu.make_async_remote_copy(
            src_ref=src,
            dst_ref=dst,
            send_sem=send,
            recv_sem=recv,
            device_id=where,
            device_id_type=MESH,
        )

    def pair_copy(src, dst, at):
        return copy_to(src, dst, x_send.at[at], x_recv.at[at], xl=1 - xl)

    def ring_block(way, step):
        back = step - 1
        return lax.rem(z + NZ - back, NZ) if way == 0 else lax.rem(z + back, NZ)

    def key_copy(way, step, piece):
        part = kbuf.at[ring_block(way, step), piece]
        return copy_to(
            part,
            part,
            ag_send.at[way, step - 1, piece],
            ag_recv.at[way, step - 1, piece],
            z=up if way == 0 else down,
        )

    def weight_copy(way, step):
        part = wfull.at[core * NZ + ring_block(way, step), :, lanes(y)]
        return copy_to(
            part,
            part,
            wz_send.at[way, step - 1],
            wz_recv.at[way, step - 1],
            z=up if way == 0 else down,
        )

    def part_copy(way, step, piece):
        return copy_to(
            rsend.at[way, step, piece],
            rrecv.at[way, step, piece],
            rs_send.at[way, step, piece],
            rs_recv.at[way, step, piece],
            z=up if way == 0 else down,
        )

    def key_pair(i):
        rows = pl.ds(pl.multiple_of(64 * (1 - xl) + 32 * i, 32), 32)
        return pair_copy(kv.at[rows], kbuf.at[z, 2 * xl + i], 5 * i)

    query_pair = pair_copy(qv.at[theirs], qst, 1)
    grad_pair = pair_copy(gsend.at[theirs], gst, 2)
    own_weight = wfull.at[core * NZ + z, :, lanes(y)]
    weight_pair = pair_copy(wv.at[:, lanes(y)], own_weight, 3)
    for i in range(2):
        key_pair(i).start()
        for way in range(2):
            key_copy(way, 1, 2 * xl + i).start()

    @pl.when(core == xl)
    def _():
        weight_pair.start()
        wfull[core * NZ + z, :, lanes(y)] = wv[:, lanes(y)]

    query_pair.start()
    hello(0, around + beside[:1] + [{"core": 1 - core}])

    for i in range(3, 9):
        loads[i].wait()
    coeff = coefficient_row(newv, oldv, rewv, gidv, lenv, side, (xl * NZ + z) * 64)
    diag = lax.broadcasted_iota(jnp.int32, (128, 128), 0) == lax.broadcasted_iota(
        jnp.int32, (128, 128), 1
    )
    coeff_col = jnp.sum(jnp.where(diag, coeff, 0.0), axis=1, keepdims=True)
    for head in range(KVH * PER):
        cols = slice(head * HEAD, (head + 1) * HEAD)
        gsend[:, cols] = (coeff_col * gv[:, cols].astype(jnp.float32)).astype(jnp.bfloat16)
    grad_pair.start()
    for i in range(2):
        key_pair(i).wait_recv()
        for way in range(2):
            key_copy(way, 1, 2 * (1 - xl) + i).start()


    @pl.when(core != xl)
    def _():
        weight_pair.wait_recv()

    for way in range(2):
        weight_copy(way, 1).start()

    def spread(dst, src, rows, half, group):
        for head in range(PER):
            at = pl.ds(pl.multiple_of(64 * half, 64) + head * 128, 64)
            col = (group * PER + head) * HEAD
            dst[group, at, :] = src[rows, col : col + HEAD]

    mrow[...] = jnp.full(mrow.shape, LOW, jnp.float32)
    lrow[...] = jnp.zeros(lrow.shape, jnp.float32)

    def arrived(step, work):
        last = isinstance(step, int) and step == 8
        for i in range(4):
            piece = lax.rem(2 * xl + i, 4)
            key_copy(0, step, piece).wait_recv()
            if last:
                work(i)
                continue
            key_copy(0, step + 1, piece).start()
            key_copy(1, step, piece).wait_recv()

            @pl.when(step < 7)
            def _():
                key_copy(1, step + 1, piece).start()

            work(i)
        weight_copy(0, step).wait_recv()
        if last:
            return
        weight_copy(0, step + 1).start()
        weight_copy(1, step).wait_recv()

        @pl.when(step < 7)
        def _():
            weight_copy(1, step + 1).start()

    loads[9].wait()

    def turn(n):
        xt[n] = xv[:, n * 640 : (n + 1) * 640].T.reshape(4, 160, 128)

    def input_copies():
        copies = []
        for step in range(4):
            for flip in range(2):
                if step + flip:
                    there = core ^ flip
                    copies.append(
                        copy_to(
                            xt.at[pl.ds(4 * there, 4), y_at(step)],
                            xg.at[:, :, lanes(2 * y + core)],
                            in_send.at[step * 2 + flip],
                            in_recv.at[step * 2 + flip],
                            y=y_at(step),
                            core=there,
                        )
                    )
        return copies

    def moment_copies():
        copies = []
        for step in range(4):
            for flip in range(4):
                if step + flip:
                    copies.append(
                        copy_to(
                            mv,
                            moms.at[side],
                            mo_send.at[step * 4 + flip],
                            mo_recv.at[step * 4 + flip],
                            y=y_at(step),
                            xh=xh ^ (flip & 1),
                            core=core ^ (flip >> 1),
                        )
                    )
        return copies

    row = lax.broadcasted_iota(jnp.int32, (256, 1), 0)
    lane = lax.broadcasted_iota(jnp.int32, (1, QB), 1)
    in_head = lax.rem(lane, 128)
    qpos = jnp.where(in_head < 64, in_head, in_head - 64 + 1024) + z * 64
    in_block = lax.rem(row, 128)
    kpos_base = jnp.where(in_block < 64, in_block, in_block - 64 + 1024)

    def score(index):
        t = index // KVH + 1
        head = lax.rem(index, KVH)
        a = lax.rem(z + NZ - t, NZ)
        b = lax.rem(z + jnp.where(t == 8, 0, t), NZ)
        keys = jnp.concatenate(
            [
                kbuf[a, :, :, lanes(head)].reshape(128, HEAD),
                kbuf[b, :, :, lanes(head)].reshape(128, HEAD),
            ],
            axis=0,
        )
        s = lax.dot_general(
            keys, qh[head], (((1,), (1,)), ((), ())), preferred_element_type=jnp.float32
        )
        kpos = kpos_base + jnp.where(row < 128, a, b) * 64
        s = jnp.where(kpos <= qpos, s, LOW)
        old = mrow[head]
        top = jnp.maximum(old, jnp.max(s, axis=0, keepdims=True))
        e = jnp.exp2((s - top) * EXP_SCALE)
        lrow[head] = lrow[head] * jnp.exp2((old - top) * EXP_SCALE) + jnp.sum(
            e, axis=0, keepdims=True
        )
        mrow[head] = top
        mst[t - 1, head] = top
        eb[t - 1, head] = e.astype(jnp.bfloat16)

    arrived(1, lambda i: spread(qh, qv, mine, xl, i))
    heard(0, range(4))
    hello(1, [{"core": 1 - core}])
    arrived(2, lambda i: turn(i))
    heard(1, range(1))
    hello(2, beside)
    arrived(3, lambda i: turn(4 + i))
    heard(2, range(2))
    hello(3, beside)
    for copy in input_copies():
        copy.start()
    query_pair.wait_recv()

    def second_half(i):
        spread(qh, qst, slice(None), 1 - xl, i)
        spread(gh, gsend, mine, xl, i)

    arrived(4, second_half)
    heard(3, range(2))
    for copy in moment_copies():
        copy.start()

    def key_step(step, carry):
        def work(i):
            for unit in range(2):
                score((step - 5) * 8 + i * 2 + unit)

        arrived(step, work)
        return carry

    lax.fori_loop(5, 8, key_step, 0)
    xg[:, :, lanes(2 * y + core)] = xt[pl.ds(4 * core, 4), y]
    grad_pair.wait_recv()

    def last_step(i):
        score(24 + i)
        spread(gh, gst, slice(None), 1 - xl, i)

    arrived(8, last_step)

    def across_y(step):
        part = wfull.at[pl.ds(NZ * core, NZ), :, lanes(y)]
        return copy_to(part, part, wy_send.at[step], wy_recv.at[step], y=y_at(step))

    def across_core():
        part = wfull.at[pl.ds(NZ * core, NZ)]
        return copy_to(part, part, wy_send.at[0], wy_recv.at[0], core=1 - core)

    for step in range(1, 4):
        across_y(step).start()
    for head in range(KVH):
        score(28 + head)

    lrow[...] = 1.0 / lrow[...]

    def parts(t, dst, head):
        scale = jnp.exp2((mst[t - 1, head] - mrow[head]) * EXP_SCALE) * lrow[head]
        p = (eb[t - 1, head].astype(jnp.float32) * scale).astype(jnp.bfloat16)
        dst[:, head * HEAD : (head + 1) * HEAD] = jnp.dot(
            p, gh[head], preferred_element_type=jnp.float32
        )

    def pass_on(way, step, src, piece, first):
        value = src[piece * 32 : (piece + 1) * 32, :]
        if not first:
            part_copy(way, step - 1, piece).wait_recv()
            value = value + rrecv[way, step - 1, piece].astype(jnp.float32)
        rsend[way, step, piece] = value.astype(jnp.bfloat16)
        part_copy(way, step, piece).start()

    for head in range(KVH):
        parts(8, pbuf.at[0], head)
    for piece in range(4):
        pass_on(0, 0, pbuf.at[0, pl.ds(0, 128)], piece, True)
    pown[...] = pbuf[0, 128:256, :]
    for head in range(KVH):
        parts(7, pbuf.at[1], head)
    for piece in range(4):
        pass_on(1, 0, pbuf.at[1, pl.ds(0, 128)], piece, True)
    for head in range(KVH):
        parts(6, pbuf.at[0], head)
    for piece in range(4):
        pass_on(0, 1, pbuf.at[1, pl.ds(128, 128)], piece, False)

    def ring_step(i, carry):
        now = pbuf.at[lax.rem(i, 2)]
        later = pbuf.at[1 - lax.rem(i, 2)]
        for piece in range(4):
            pass_on(1, i - 1, now.at[pl.ds(0, 128)], piece, False)
            pass_on(0, i, now.at[pl.ds(128, 128)], piece, False)
            parts(7 - i, later, piece)
        return carry

    lax.fori_loop(2, 7, ring_step, 0)
    for piece in range(4):
        pass_on(1, 6, pbuf.at[1, pl.ds(0, 128)], piece, False)
        pass_on(0, 7, pbuf.at[1, pl.ds(128, 128)], piece, False)

    for copy in moment_copies():
        copy.wait_recv()
    for s in range(16):
        m1f[10 * s : 10 * s + 10, :] = moms[s, 0:10, :].astype(jnp.float32)
        m2f[10 * s : 10 * s + 10, :] = moms[s, 16:26, :].astype(jnp.float32)

    value_pair = pair_copy(vsend, vrecv, 4)
    for piece in range(4):
        part_copy(1, 6, piece).wait_recv()
        part_copy(0, 7, piece).wait_recv()

    def block_rows(half):
        rows = pl.ds(2 * half, 2)
        return (
            pown[pl.ds(pl.multiple_of(64 * half, 64), 64), :]
            + rrecv[1, 6, rows].reshape(64, 512).astype(jnp.float32)
            + rrecv[0, 7, rows].reshape(64, 512).astype(jnp.float32)
        ).astype(jnp.bfloat16)

    vsend[...] = block_rows(1 - xl)
    value_pair.start()
    slot = 2 * y + core
    vga[slot, mine, :] = block_rows(xl)
    value_pair.wait_recv()
    vga[slot, theirs, :] = vrecv[...]

    def values_y(step):
        return copy_to(vga.at[slot], vga.at[slot], va_send.at[step], va_recv.at[step], y=y_at(step))

    def values_core(step):
        part = vga.at[2 * lax.rem(y + 4 - step, 4) + core]
        return copy_to(part, part, va_send.at[4 + step], va_recv.at[4 + step], core=1 - core)

    for step in (2, 1, 3):
        values_y(step).start()
    values_core(0).start()

    for copy in input_copies():
        copy.wait_recv()
    for step in range(1, 4):
        across_y(step).wait_recv()
    across_core().start()

    def add_inputs(step, first):
        at = lax.rem(y + 4 - step, 4)
        a = xg[:, :, pl.ds(pl.multiple_of(at * 256, 256), 256)].reshape(640, 256)
        b = vga[pl.ds(2 * at, 2)].reshape(256, 512)
        value = jnp.dot(a, b, preferred_element_type=jnp.float32)
        acc[...] = value if first else acc[...] + value

    values_core(0).wait_recv()
    add_inputs(0, True)
    for step in (1, 3, 2):
        values_y(step).wait_recv()
        values_core(step).start()
        values_core(step).wait_recv()
        add_inputs(step, False)

    def sum_x(step, half):
        at = lax.rem(x + step, 4)
        rows = pl.ds(320 * half, 320)
        return copy_to(
            xs.at[step - 1, rows],
            xr.at[step - 1, rows],
            xs_send.at[step - 1, half],
            xs_recv.at[step - 1, half],
            xl=lax.rem(at, 2),
            xh=at // 2,
        )

    for half in range(2):
        rows = pl.ds(320 * half, 320)
        for step in (2, 1, 3):
            at = lax.rem(x + step, 4)
            xs[step - 1, rows] = acc[rows, lanes(at)].astype(jnp.bfloat16)
            sum_x(step, half).start()

    across_core().wait_recv()

    def grad_tile(n, carry):
        w = wfull[pl.ds(4 * n, 4)].reshape(640, 512)
        ig_ref[:, pl.ds(pl.multiple_of(n * 640, 128), 640)] = lax.dot_general(
            vga[slot], w, (((1,), (1,)), ((), ())), preferred_element_type=jnp.float32
        ).astype(jnp.bfloat16)
        return carry

    lax.fori_loop(0, 8, grad_tile, 0)

    def sum_z(j):
        at = 4 * j + y
        far = lax.rem(z - at + NZ, NZ)
        return copy_to(zs.at[j], zr.at[far], zs_send.at[j], zs_recv.at[far], z=at)

    for half in range(2):
        rows = pl.ds(320 * half, 320)
        total = acc[rows, lanes(x)]
        for step in (1, 3, 2):
            sum_x(step, half).wait_recv()
            total = total + xr[step - 1, rows].astype(jnp.float32)
        zsum[2 * half : 2 * half + 2] = total.reshape(2, 160, 128)
        zs[2 * half : 2 * half + 2] = total.reshape(2, 160, 128).astype(jnp.bfloat16)
        for j in range(2 * half, 2 * half + 2):

            @pl.when(z != 4 * j + y)
            def _(j=j):
                sum_z(j).start()

    root = lax.rem(z, 4) == y

    def spread_y(step):
        return copy_to(gy, gy, gy_send.at[step - 1], gy_recv, y=y_at(step))

    @pl.when(root)
    def _():
        total = zsum[z // 4]
        for far in range(1, NZ):
            copy_to(zs.at[0], zr.at[far], zs_send.at[0], zs_recv.at[far], z=up).wait_recv()
            total = total + zr[far].astype(jnp.float32)
        gy[...] = total.astype(jnp.bfloat16)
        for step in range(1, 4):
            spread_y(step).start()

    @pl.when(jnp.logical_not(root))
    def _():
        spread_y(1).wait_recv()

    def spread_x(to_xh, to_core):
        k = to_xh * 2 + to_core
        return copy_to(
            gy, gf.at[x], gf_send.at[k], gf_recv.at[x], xl=core, xh=to_xh, core=to_core
        )

    def is_self(to_xh, to_core):
        return (xl == core) & (xh == to_xh) & (core == to_core)

    for to_xh in range(2):
        for to_core in range(2):

            @pl.when(jnp.logical_not(is_self(to_xh, to_core)))
            def _(to_xh=to_xh, to_core=to_core):
                spread_x(to_xh, to_core).start()

    @pl.when(xl == core)
    def _():
        gf[x] = gy[...]

    for at in range(4):

        @pl.when(jnp.logical_not((xl == core) & (x == at)))
        def _(at=at):
            copy_to(gy, gf.at[at], gf_send.at[0], gf_recv.at[at], core=1 - core).wait_recv()

    for at in range(4):
        cols = slice(at * 128, (at + 1) * 128)
        new, first, second = adam_rows(
            wv[:, cols].astype(jnp.float32),
            gf[at].astype(jnp.float32),
            m1f[:, cols],
            m2f[:, cols],
        )
        np_ref[:, cols] = new.astype(jnp.bfloat16)
        m1f[:, cols] = first
        m2f[:, cols] = second
    for s in range(16):

        @pl.when(side == s)
        def _(s=s):
            nf_ref[...] = m1f[10 * s : 10 * s + 10, :].astype(jnp.bfloat16)
            ns_ref[...] = m2f[10 * s : 10 * s + 10, :].astype(jnp.bfloat16)

    for way in range(2):
        for step in range(8 - way):
            weight_copy(way, step + 1).wait_send()
            for piece in range(4):
                key_copy(way, step + 1, piece).wait_send()
                part_copy(way, step, piece).wait_send()
    for copy in (key_pair(0), key_pair(1), query_pair, grad_pair, value_pair):
        copy.wait_send()

    @pl.when(core == xl)
    def _():
        weight_pair.wait_send()

    for copy in input_copies() + moment_copies():
        copy.wait_send()
    across_core().wait_send()
    values_core(0).wait_send()
    for step in range(1, 4):
        across_y(step).wait_send()
        values_y(step).wait_send()
        values_core(step).wait_send()
        for half in range(2):
            sum_x(step, half).wait_send()
    for j in range(4):

        @pl.when(z != 4 * j + y)
        def _(j=j):
            sum_z(j).wait_send()

    @pl.when(root)
    def _():
        for step in range(1, 4):
            spread_y(step).wait_send()

    for to_xh in range(2):
        for to_core in range(2):

            @pl.when(jnp.logical_not(is_self(to_xh, to_core)))
            def _(to_xh=to_xh, to_core=to_core):
                spread_x(to_xh, to_core).wait_send()


def shards(
    attn_inputs,
    queries,
    key_vectors,
    logp_grad,
    new_logp,
    old_logp,
    rewards,
    group_ids,
    lengths,
    value_proj,
    first_moment,
    second_moment,
):
    vmem = pl.BlockSpec(memory_space=pltpu.VMEM)
    hbm = pl.BlockSpec(memory_space=pl.ANY)
    dma = pltpu.SemaphoreType.DMA
    bf, f32, i32 = jnp.bfloat16, jnp.float32, jnp.int32

    def buf(*shape, kind=bf):
        return pltpu.VMEM(shape, kind)

    return pl.pallas_call(
        kernel,
        out_shape=(
            jax.ShapeDtypeStruct((128, 5120), bf),
            jax.ShapeDtypeStruct((160, 512), bf),
            jax.ShapeDtypeStruct((10, 512), bf),
            jax.ShapeDtypeStruct((10, 512), bf),
        ),
        in_specs=[hbm] * 10 + [vmem] * 2,
        out_specs=(vmem,) * 4,
        scratch_shapes=[
            buf(128, 2560),
            buf(128, 2560),
            buf(128, 512),
            buf(128, 5120),
            buf(160, 512),
            buf(1, 128, kind=f32),
            buf(1, 128, kind=f32),
            buf(1, 32, kind=f32),
            buf(1, 32, kind=i32),
            buf(1, 32, kind=i32),
            buf(NZ, 4, 32, 512),
            buf(128, 2560),
            buf(64, 2560),
            buf(64, 2560),
            buf(KVH, QB, HEAD),
            buf(KVH, QB, HEAD),
            buf(8, KVH, 256, QB),
            buf(8, KVH, 1, QB, kind=f32),
            buf(KVH, 1, QB, kind=f32),
            buf(KVH, 1, QB, kind=f32),
            buf(2, 256, 512, kind=f32),
            buf(128, 512, kind=f32),
            buf(2, 8, 4, 32, 512),
            buf(2, 8, 4, 32, 512),
            buf(64, 512),
            buf(64, 512),
            buf(8, 4, 160, 128),
            buf(4, 160, 1024),
            buf(32, 160, 512),
            buf(32, 512),
            buf(16, 32, 512),
            buf(160, 512, kind=f32),
            buf(160, 512, kind=f32),
            buf(8, 128, 512),
            buf(640, 512, kind=f32),
            buf(3, 640, 128),
            buf(3, 640, 128),
            buf(4, 160, 128, kind=f32),
            buf(4, 160, 128),
            buf(NZ, 160, 128),
            buf(160, 128),
            buf(4, 160, 128),
            dma((10,)),
            dma((6,)),
            dma((6,)),
            dma((2, 8, 4)),
            dma((2, 8, 4)),
            dma((2, 8, 4)),
            dma((2, 8, 4)),
            dma((8,)),
            dma((8,)),
            dma((2, 8)),
            dma((2, 8)),
            dma((4,)),
            dma((4,)),
            dma((16,)),
            dma((16,)),
            dma((8,)),
            dma((8,)),
            dma((3, 2)),
            dma((3, 2)),
            dma((4,)),
            dma((16,)),
            dma((3,)),
            dma,
            dma((4,)),
            dma((4,)),
            pltpu.SemaphoreType.REGULAR((4,)),
        ],
        compiler_params=pltpu.CompilerParams(
            collective_id=0, has_side_effects=True, vmem_limit_bytes=60 * 1024 * 1024
        ),
    )(
        attn_inputs,
        queries,
        key_vectors,
        logp_grad,
        new_logp.reshape(1, 128),
        old_logp.reshape(1, 128),
        rewards.reshape(1, 32),
        group_ids.reshape(1, 32),
        lengths.reshape(1, 32),
        value_proj,
        first_moment,
        second_moment,
    )


def solution(mesh):
    torus = Mesh(mesh.devices.reshape(2, 16, 4, 2, 2), AXES)
    placed = (
        P(SIDE_FSDP, None),
        P(SIDE_FSDP, None),
        P(SIDE_FSDP, None),
        P(SIDE_FSDP, None),
        P(SIDE_FSDP),
        P(SIDE_FSDP),
        P(),
        P(),
        P(),
        P(FSDP, None),
        P(FSDP_SIDE, None),
        P(FSDP_SIDE, None),
    )
    return jax.shard_map(
        shards,
        mesh=torus,
        in_specs=placed,
        out_specs=(P(SIDE_FSDP, None), P(FSDP, None), P(FSDP_SIDE, None), P(FSDP_SIDE, None)),
        check_vma=False,
    )
```

```python
import math

import jax
import jax.numpy as jnp
from jax import lax
from jax.experimental import pallas as pl
from jax.experimental.pallas import tpu as pltpu
from jax.sharding import Mesh
from jax.sharding import PartitionSpec as P

AXES = ("xl", "z", "y", "xh", "core")
FSDP = ("xl", "z")
SIDE = ("y", "xh", "core")
SIDE_FSDP = SIDE + FSDP
FSDP_SIDE = FSDP + SIDE
MESH = pl.DeviceIdType.MESH
NZ = 16
KVH = 4
PER = 5
HEAD = 128
QB = PER * 128
EXP_SCALE = math.log2(math.e) / math.sqrt(HEAD)
LOW = -1e30

clip_low = 0.8
clip_high = 1.2
decay_first = 0.9
decay_second = 0.95
step_rate = 0.001
weight_decay = 0.1
adam_eps = 1e-08
bias_first = 1.0 - 0.9**10
bias_second = 1.0 - 0.95**10


def coefficient_row(new_ref, old_ref, rew_ref, gid_ref, len_ref, side, first_pos):
    rew = rew_ref[...]
    gid = gid_ref[...]
    lens = len_ref[...]
    roll_of = lax.broadcasted_iota(jnp.int32, rew.shape, 1)
    adv_parts, len_parts = [], []
    for roll in range(2):
        own = roll_of == side * 2 + roll
        own_gid = jnp.sum(jnp.where(own, gid, 0), axis=1, keepdims=True)
        own_rew = jnp.sum(jnp.where(own, rew, 0.0), axis=1, keepdims=True)
        own_len = jnp.sum(jnp.where(own, lens, 0), axis=1, keepdims=True)
        member = jnp.where(gid == own_gid, 1.0, 0.0)
        count = jnp.maximum(jnp.sum(member, axis=1, keepdims=True), 1.0)
        mean = jnp.sum(member * rew, axis=1, keepdims=True) / count
        spread = rew - mean
        var = jnp.sum(member * (spread * spread), axis=1, keepdims=True) / count
        adv_parts.append((own_rew - mean) / jnp.maximum(jnp.sqrt(var), 1.0))
        len_parts.append(own_len)
    slot = lax.broadcasted_iota(jnp.int32, (1, 128), 1)
    first = slot < 64
    adv = jnp.where(first, adv_parts[0], adv_parts[1])
    length = jnp.where(first, len_parts[0], len_parts[1])
    pos = first_pos + jnp.where(first, slot, slot - 64)
    ratio = jnp.exp(new_ref[...] - old_ref[...])
    clipped = jnp.minimum(jnp.maximum(ratio, clip_low), clip_high)
    active = (ratio * adv <= clipped * adv) & (pos < length)
    return jnp.where(active, -adv * ratio * (2048.0 / length.astype(jnp.float32)), 0.0)


def adam_rows(weight_now, grad_rows, first_moment, second_moment):
    first = decay_first * first_moment + (1.0 - decay_first) * grad_rows
    second = decay_second * second_moment + (1.0 - decay_second) * grad_rows * grad_rows
    update = (
        first / bias_first / (jnp.sqrt(second / bias_second) + adam_eps) + weight_decay * weight_now
    )
    return weight_now - step_rate * update, first, second


def kernel(
    x_hbm,
    q_hbm,
    k_hbm,
    g_hbm,
    new_hbm,
    old_hbm,
    rew_hbm,
    gid_hbm,
    len_hbm,
    w_hbm,
    m1_ref,
    m2_ref,
    ig_ref,
    np_ref,
    nf_ref,
    ns_ref,
    qv,
    gv,
    kv,
    xv,
    wv,
    newv,
    oldv,
    rewv,
    gidv,
    lenv,
    kbuf,
    gsend,
    qst,
    gst,
    qh,
    gh,
    eb,
    mst,
    mrow,
    lrow,
    pbuf,
    pown,
    rsend,
    rrecv,
    vsend,
    igv,
    xt,
    xg,
    wfull,
    mv,
    moms,
    m1f,
    m2f,
    vga,
    acc,
    xs,
    xr,
    zsum,
    zs,
    zr,
    gy,
    gf,
    load_sem,
    x_send,
    x_recv,
    ag_send,
    ag_recv,
    rs_send,
    rs_recv,
    in_send,
    in_recv,
    wz_send,
    wz_recv,
    wy_send,
    wy_recv,
    mo_send,
    mo_recv,
    va_send,
    va_recv,
    xs_send,
    xs_recv,
    zs_send,
    zs_recv,
    gy_send,
    gy_recv,
    gf_send,
    gf_recv,
    known,
):
    xl = lax.axis_index("xl")
    z = lax.axis_index("z")
    y = lax.axis_index("y")
    xh = lax.axis_index("xh")
    core = lax.axis_index("core")
    side = (y * 2 + xh) * 2 + core
    x = xh * 2 + xl
    up = lax.rem(z + 1, NZ)
    down = lax.rem(z + NZ - 1, NZ)
    mine = pl.ds(pl.multiple_of(64 * xl, 64), 64)
    theirs = pl.ds(pl.multiple_of(64 * (1 - xl), 64), 64)

    def lanes(index):
        return pl.ds(pl.multiple_of(index * 128, 128), 128)

    def y_at(step):
        return lax.rem(y + step, 4)

    loads = [
        pltpu.make_async_copy(src, dst, load_sem.at[i])
        for i, (src, dst) in enumerate(
            (
                (k_hbm, kv),
                (q_hbm, qv),
                (w_hbm, wv),
                (new_hbm, newv),
                (old_hbm, oldv),
                (rew_hbm, rewv),
                (gid_hbm, gidv),
                (len_hbm, lenv),
                (g_hbm, gv),
                (x_hbm, xv),
            )
        )
    ]
    loads[0].start()
    barrier = pltpu.get_barrier_semaphore()

    def greet(**where):
        pl.semaphore_signal(barrier, inc=1, device_id=where, device_id_type=MESH)

    beside = [{"xl": 1 - xl, "xh": xh}, {"xl": 1 - xl, "xh": 1 - xh}]
    around = [{"y": y_at(1)}, {"y": y_at(3)}]
    greet(z=up)
    greet(z=down)
    greet(**beside[0])
    greet(core=1 - core)
    for where in around + beside[1:]:
        greet(**where)

    def hello(kind, to):
        for where in to:
            pl.semaphore_signal(known.at[kind], inc=1, device_id=where, device_id_type=MESH)

    def heard(kind, to):
        pl.semaphore_wait(known.at[kind], len(to))

    for load in loads[1:]:
        load.start()
    loads[0].wait()
    kbuf[z, pl.ds(2 * xl, 2)] = kv[mine, :].reshape(2, 32, 512)
    pl.semaphore_wait(barrier, 7)

    def copy_to(src, dst, send, recv, **where):
        return pltpu.make_async_remote_copy(
            src_ref=src,
            dst_ref=dst,
            send_sem=send,
            recv_sem=recv,
            device_id=where,
            device_id_type=MESH,
        )

    def pair_copy(src, dst, at):
        return copy_to(src, dst, x_send.at[at], x_recv.at[at], xl=1 - xl)

    def ring_block(way, step):
        back = step - 1
        return lax.rem(z + NZ - back, NZ) if way == 0 else lax.rem(z + back, NZ)

    def key_copy(way, step, piece):
        part = kbuf.at[ring_block(way, step), piece]
        return copy_to(
            part,
            part,
            ag_send.at[way, step - 1, piece],
            ag_recv.at[way, step - 1, piece],
            z=up if way == 0 else down,
        )

    def weight_copy(way, step):
        part = wfull.at[core * NZ + ring_block(way, step), :, lanes(y)]
        return copy_to(
            part,
            part,
            wz_send.at[way, step - 1],
            wz_recv.at[way, step - 1],
            z=up if way == 0 else down,
        )

    def part_copy(way, step, piece):
        return copy_to(
            rsend.at[way, step, piece],
            rrecv.at[way, step, piece],
            rs_send.at[way, step, piece],
            rs_recv.at[way, step, piece],
            z=up if way == 0 else down,
        )

    def key_pair(i):
        rows = pl.ds(pl.multiple_of(64 * (1 - xl) + 32 * i, 32), 32)
        return pair_copy(kv.at[rows], kbuf.at[z, 2 * xl + i], 5 * i)

    query_pair = pair_copy(qv.at[theirs], qst, 1)
    grad_pair = pair_copy(gsend.at[theirs], gst, 2)
    own_weight = wfull.at[core * NZ + z, :, lanes(y)]
    weight_pair = pair_copy(wv.at[:, lanes(y)], own_weight, 3)
    for i in range(2):
        key_pair(i).start()
        for way in range(2):
            key_copy(way, 1, 2 * xl + i).start()
    for i in range(1, 3):
        loads[i].wait()

    @pl.when(core == xl)
    def _():
        weight_pair.start()
        wfull[core * NZ + z, :, lanes(y)] = wv[:, lanes(y)]

    query_pair.start()
    hello(0, around + beside[:1] + [{"core": 1 - core}])

    for i in range(3, 9):
        loads[i].wait()
    coeff = coefficient_row(newv, oldv, rewv, gidv, lenv, side, (xl * NZ + z) * 64)
    diag = lax.broadcasted_iota(jnp.int32, (128, 128), 0) == lax.broadcasted_iota(
        jnp.int32, (128, 128), 1
    )
    coeff_col = jnp.sum(jnp.where(diag, coeff, 0.0), axis=1, keepdims=True)
    for head in range(KVH * PER):
        cols = slice(head * HEAD, (head + 1) * HEAD)
        gsend[:, cols] = (coeff_col * gv[:, cols].astype(jnp.float32)).astype(jnp.bfloat16)
    grad_pair.start()
    for i in range(2):
        key_pair(i).wait_recv()
        for way in range(2):
            key_copy(way, 1, 2 * (1 - xl) + i).start()


    @pl.when(core != xl)
    def _():
        weight_pair.wait_recv()

    for way in range(2):
        weight_copy(way, 1).start()

    def spread(dst, src, rows, half, group):
        for head in range(PER):
            at = pl.ds(pl.multiple_of(64 * half, 64) + head * 128, 64)
            col = (group * PER + head) * HEAD
            dst[group, at, :] = src[rows, col : col + HEAD]

    mrow[...] = jnp.full(mrow.shape, LOW, jnp.float32)
    lrow[...] = jnp.zeros(lrow.shape, jnp.float32)

    def arrived(step, work):
        last = isinstance(step, int) and step == 8
        for i in range(4):
            piece = lax.rem(2 * xl + i, 4)
            key_copy(0, step, piece).wait_recv()
            if last:
                work(i)
                continue
            key_copy(0, step + 1, piece).start()
            key_copy(1, step, piece).wait_recv()

            @pl.when(step < 7)
            def _():
                key_copy(1, step + 1, piece).start()

            work(i)
        weight_copy(0, step).wait_recv()
        if last:
            return
        weight_copy(0, step + 1).start()
        weight_copy(1, step).wait_recv()

        @pl.when(step < 7)
        def _():
            weight_copy(1, step + 1).start()

    loads[9].wait()

    def turn(n):
        xt[n] = xv[:, n * 640 : (n + 1) * 640].T.reshape(4, 160, 128)

    def input_copies():
        copies = []
        for step in range(4):
            for flip in range(2):
                if step + flip:
                    there = core ^ flip
                    copies.append(
                        copy_to(
                            xt.at[pl.ds(4 * there, 4), y_at(step)],
                            xg.at[:, :, lanes(2 * y + core)],
                            in_send.at[step * 2 + flip],
                            in_recv.at[step * 2 + flip],
                            y=y_at(step),
                            core=there,
                        )
                    )
        return copies

    def moment_copies():
        copies = []
        for step in range(4):
            for flip in range(4):
                if step + flip:
                    copies.append(
                        copy_to(
                            mv,
                            moms.at[side],
                            mo_send.at[step * 4 + flip],
                            mo_recv.at[step * 4 + flip],
                            y=y_at(step),
                            xh=xh ^ (flip & 1),
                            core=core ^ (flip >> 1),
                        )
                    )
        return copies

    mv[...] = jnp.zeros(mv.shape, mv.dtype)
    mv[0:10, :] = m1_ref[...]
    mv[16:26, :] = m2_ref[...]
    moms[side] = mv[...]

    row = lax.broadcasted_iota(jnp.int32, (256, 1), 0)
    lane = lax.broadcasted_iota(jnp.int32, (1, QB), 1)
    in_head = lax.rem(lane, 128)
    qpos = jnp.where(in_head < 64, in_head, in_head - 64 + 1024) + z * 64
    in_block = lax.rem(row, 128)
    kpos_base = jnp.where(in_block < 64, in_block, in_block - 64 + 1024)

    def score(index):
        t = index // KVH + 1
        head = lax.rem(index, KVH)
        a = lax.rem(z + NZ - t, NZ)
        b = lax.rem(z + jnp.where(t == 8, 0, t), NZ)
        keys = jnp.concatenate(
            [
                kbuf[a, :, :, lanes(head)].reshape(128, HEAD),
                kbuf[b, :, :, lanes(head)].reshape(128, HEAD),
            ],
            axis=0,
        )
        s = lax.dot_general(
            keys, qh[head], (((1,), (1,)), ((), ())), preferred_element_type=jnp.float32
        )
        kpos = kpos_base + jnp.where(row < 128, a, b) * 64
        s = jnp.where(kpos <= qpos, s, LOW)
        old = mrow[head]
        top = jnp.maximum(old, jnp.max(s, axis=0, keepdims=True))
        e = jnp.exp2((s - top) * EXP_SCALE)
        lrow[head] = lrow[head] * jnp.exp2((old - top) * EXP_SCALE) + jnp.sum(
            e, axis=0, keepdims=True
        )
        mrow[head] = top
        mst[t - 1, head] = top
        eb[t - 1, head] = e.astype(jnp.bfloat16)

    arrived(1, lambda i: spread(qh, qv, mine, xl, i))
    heard(0, range(4))
    hello(1, [{"core": 1 - core}])
    arrived(2, lambda i: turn(i))
    heard(1, range(1))
    hello(2, beside)
    arrived(3, lambda i: turn(4 + i))
    heard(2, range(2))
    hello(3, beside)
    for copy in input_copies():
        copy.start()
    query_pair.wait_recv()

    def second_half(i):
        spread(qh, qst, slice(None), 1 - xl, i)
        spread(gh, gsend, mine, xl, i)

    arrived(4, second_half)
    heard(3, range(2))
    for copy in moment_copies():
        copy.start()

    def key_step(step, carry):
        def work(i):
            for unit in range(2):
                score((step - 5) * 8 + i * 2 + unit)

        arrived(step, work)
        return carry

    lax.fori_loop(5, 8, key_step, 0)
    xg[:, :, lanes(2 * y + core)] = xt[pl.ds(4 * core, 4), y]
    grad_pair.wait_recv()

    def last_step(i):
        score(24 + i)
        spread(gh, gst, slice(None), 1 - xl, i)

    arrived(8, last_step)

    def across_y(step):
        part = wfull.at[pl.ds(NZ * core, NZ), :, lanes(y)]
        return copy_to(part, part, wy_send.at[step], wy_recv.at[step], y=y_at(step))

    def across_core():
        part = wfull.at[pl.ds(NZ * core, NZ)]
        return copy_to(part, part, wy_send.at[0], wy_recv.at[0], core=1 - core)

    for step in range(1, 4):
        across_y(step).start()
    for head in range(KVH):
        score(28 + head)

    lrow[...] = 1.0 / lrow[...]

    def parts(t, dst, head):
        scale = jnp.exp2((mst[t - 1, head] - mrow[head]) * EXP_SCALE) * lrow[head]
        p = (eb[t - 1, head].astype(jnp.float32) * scale).astype(jnp.bfloat16)
        dst[:, head * HEAD : (head + 1) * HEAD] = jnp.dot(
            p, gh[head], preferred_element_type=jnp.float32
        )

    def pass_on(way, step, src, piece, first):
        piece = lax.rem(piece + 2 * (1 - xl), 4)
        value = src[pl.ds(pl.multiple_of(piece * 32, 32), 32), :]
        if not first:
            part_copy(way, step - 1, piece).wait_recv()
            value = value + rrecv[way, step - 1, piece].astype(jnp.float32)
        rsend[way, step, piece] = value.astype(jnp.bfloat16)
        part_copy(way, step, piece).start()

    for head in range(KVH):
        parts(8, pbuf.at[0], head)
    for piece in range(4):
        pass_on(0, 0, pbuf.at[0, pl.ds(0, 128)], piece, True)
    pown[...] = pbuf[0, 128:256, :]
    for head in range(KVH):
        parts(7, pbuf.at[1], head)
    for piece in range(4):
        pass_on(1, 0, pbuf.at[1, pl.ds(0, 128)], piece, True)
    for head in range(KVH):
        parts(6, pbuf.at[0], head)
    for piece in range(4):
        pass_on(0, 1, pbuf.at[1, pl.ds(128, 128)], piece, False)

    def ring_step(i, carry):
        now = pbuf.at[lax.rem(i, 2)]
        later = pbuf.at[1 - lax.rem(i, 2)]
        for piece in range(4):
            pass_on(1, i - 1, now.at[pl.ds(0, 128)], piece, False)
            pass_on(0, i, now.at[pl.ds(128, 128)], piece, False)
            parts(7 - i, later, piece)
        return carry

    lax.fori_loop(2, 7, ring_step, 0)
    for piece in range(4):
        pass_on(1, 6, pbuf.at[1, pl.ds(0, 128)], piece, False)
        pass_on(0, 7, pbuf.at[1, pl.ds(128, 128)], piece, False)

    slot = 2 * y + core
    value_pair = pair_copy(vsend, vga.at[slot, mine], 4)

    def block_rows(half):
        for i in range(2):
            part_copy(1, 6, 2 * half + i).wait_recv()
            part_copy(0, 7, 2 * half + i).wait_recv()
        rows = pl.ds(2 * half, 2)
        return (
            pown[pl.ds(pl.multiple_of(64 * half, 64), 64), :]
            + rrecv[1, 6, rows].reshape(64, 512).astype(jnp.float32)
            + rrecv[0, 7, rows].reshape(64, 512).astype(jnp.float32)
        ).astype(jnp.bfloat16)

    def value_part(at, part):
        return vga.at[at, theirs if part else mine]

    def values_y(step, part):
        rows = value_part(slot, part)
        return copy_to(
            rows, rows, va_send.at[step, part], va_recv.at[step, part], y=y_at(step)
        )

    def values_core(step, part):
        rows = value_part(2 * lax.rem(y + 4 - step, 4) + core, part)
        return copy_to(
            rows, rows, va_send.at[4 + step, part], va_recv.at[4 + step, part], core=1 - core
        )

    vsend[...] = block_rows(1 - xl)
    value_pair.start()
    vga[slot, mine, :] = block_rows(xl)
    for step in (2, 1, 3):
        values_y(step, 0).start()
    values_core(0, 0).start()
    value_pair.wait_recv()
    for step in (2, 1, 3):
        values_y(step, 1).start()
    values_core(0, 1).start()

    for copy in input_copies():
        copy.wait_recv()

    def add_inputs(step, first):
        at = lax.rem(y + 4 - step, 4)
        a = xg[:, :, pl.ds(pl.multiple_of(at * 256, 256), 256)].reshape(640, 256)
        b = vga[pl.ds(2 * at, 2)].reshape(256, 512)
        value = jnp.dot(a, b, preferred_element_type=jnp.float32)
        acc[...] = value if first else acc[...] + value

    for step in (1, 3, 2):
        values_y(step, 0).wait_recv()
        values_core(step, 0).start()
    for part in range(2):
        values_core(0, part).wait_recv()
    add_inputs(0, True)
    for step in (1, 3, 2):
        values_y(step, 1).wait_recv()
        values_core(step, 1).start()
        for part in range(2):
            values_core(step, part).wait_recv()
        add_inputs(step, False)

    def sum_x(step, half):
        at = lax.rem(x + step, 4)
        rows = pl.ds(320 * half, 320)
        return copy_to(
            xs.at[step - 1, rows],
            xr.at[step - 1, rows],
            xs_send.at[step - 1, half],
            xs_recv.at[step - 1, half],
            xl=lax.rem(at, 2),
            xh=at // 2,
        )

    for half in range(2):
        rows = pl.ds(320 * half, 320)
        for step in (2, 1, 3):
            at = lax.rem(x + step, 4)
            xs[step - 1, rows] = acc[rows, lanes(at)].astype(jnp.bfloat16)
            sum_x(step, half).start()

    for step in range(1, 4):
        across_y(step).wait_recv()
    across_core().start()

    for copy in moment_copies():
        copy.wait_recv()
    for s in range(16):
        m1f[10 * s : 10 * s + 10, :] = moms[s, 0:10, :].astype(jnp.float32)
        m2f[10 * s : 10 * s + 10, :] = moms[s, 16:26, :].astype(jnp.float32)

    for way in range(2):
        for step in range(8 - way):
            weight_copy(way, step + 1).wait_send()
            for piece in range(4):
                key_copy(way, step + 1, piece).wait_send()
    for copy in [key_pair(0), key_pair(1), query_pair, grad_pair] + input_copies():
        copy.wait_send()

    @pl.when(core == xl)
    def _():
        weight_pair.wait_send()

    def sum_z(j):
        at = 4 * j + y
        far = lax.rem(z - at + NZ, NZ)
        return copy_to(zs.at[j], zr.at[far], zs_send.at[j], zs_recv.at[far], z=at)

    for half in range(2):
        rows = pl.ds(320 * half, 320)
        total = acc[rows, lanes(x)]
        for step in (1, 3, 2):
            sum_x(step, half).wait_recv()
            total = total + xr[step - 1, rows].astype(jnp.float32)
        zsum[2 * half : 2 * half + 2] = total.reshape(2, 160, 128)
        zs[2 * half : 2 * half + 2] = total.reshape(2, 160, 128).astype(jnp.bfloat16)
        for j in range(2 * half, 2 * half + 2):

            @pl.when(z != 4 * j + y)
            def _(j=j):
                sum_z(j).start()

    across_core().wait_recv()

    def grad_tile(n, carry):
        w = wfull[pl.ds(4 * n, 4)].reshape(640, 512)
        igv[:, pl.ds(pl.multiple_of(n * 640, 128), 640)] = lax.dot_general(
            vga[slot], w, (((1,), (1,)), ((), ())), preferred_element_type=jnp.float32
        ).astype(jnp.bfloat16)
        return carry

    lax.fori_loop(0, 8, grad_tile, 0)
    grad_out = [
        pltpu.make_async_copy(igv.at[pl.ds(32 * i, 32)], ig_ref.at[pl.ds(32 * i, 32)], load_sem.at[i])
        for i in range(4)
    ]
    for out in grad_out:
        out.start()
    for way in range(2):
        for step in range(8 - way):
            for piece in range(4):
                part_copy(way, step, piece).wait_send()
    value_pair.wait_send()
    for copy in moment_copies():
        copy.wait_send()
    for step in range(1, 4):
        across_y(step).wait_send()
        for half in range(2):
            values_y(step, half).wait_send()
            sum_x(step, half).wait_send()
    for step in range(4):
        for part in range(2):
            values_core(step, part).wait_send()

    root = lax.rem(z, 4) == y

    def spread_y(step):
        return copy_to(gy, gy, gy_send.at[step - 1], gy_recv, y=y_at(step))

    @pl.when(root)
    def _():
        total = zsum[z // 4]
        for far in range(1, NZ):
            copy_to(zs.at[0], zr.at[far], zs_send.at[0], zs_recv.at[far], z=up).wait_recv()
            total = total + zr[far].astype(jnp.float32)
        gy[...] = total.astype(jnp.bfloat16)
        for step in range(1, 4):
            spread_y(step).start()

    @pl.when(jnp.logical_not(root))
    def _():
        spread_y(1).wait_recv()

    def spread_x(to_xh, to_core):
        k = to_xh * 2 + to_core
        return copy_to(
            gy, gf.at[x], gf_send.at[k], gf_recv.at[x], xl=core, xh=to_xh, core=to_core
        )

    def is_self(to_xh, to_core):
        return (xl == core) & (xh == to_xh) & (core == to_core)

    for to_xh in range(2):
        for to_core in range(2):

            @pl.when(jnp.logical_not(is_self(to_xh, to_core)))
            def _(to_xh=to_xh, to_core=to_core):
                spread_x(to_xh, to_core).start()

    @pl.when(xl == core)
    def _():
        gf[x] = gy[...]

    for at in range(4):

        @pl.when(jnp.logical_not((xl == core) & (x == at)))
        def _(at=at):
            copy_to(gy, gf.at[at], gf_send.at[0], gf_recv.at[at], core=1 - core).wait_recv()

        cols = slice(at * 128, (at + 1) * 128)
        new, first, second = adam_rows(
            wv[:, cols].astype(jnp.float32),
            gf[at].astype(jnp.float32),
            m1f[:, cols],
            m2f[:, cols],
        )
        np_ref[:, cols] = new.astype(jnp.bfloat16)
        m1f[:, cols] = first
        m2f[:, cols] = second
    for s in range(16):

        @pl.when(side == s)
        def _(s=s):
            nf_ref[...] = m1f[10 * s : 10 * s + 10, :].astype(jnp.bfloat16)
            ns_ref[...] = m2f[10 * s : 10 * s + 10, :].astype(jnp.bfloat16)

    across_core().wait_send()
    for out in grad_out:
        out.wait()
    for j in range(4):

        @pl.when(z != 4 * j + y)
        def _(j=j):
            sum_z(j).wait_send()

    @pl.when(root)
    def _():
        for step in range(1, 4):
            spread_y(step).wait_send()

    for to_xh in range(2):
        for to_core in range(2):

            @pl.when(jnp.logical_not(is_self(to_xh, to_core)))
            def _(to_xh=to_xh, to_core=to_core):
                spread_x(to_xh, to_core).wait_send()


def shards(
    attn_inputs,
    queries,
    key_vectors,
    logp_grad,
    new_logp,
    old_logp,
    rewards,
    group_ids,
    lengths,
    value_proj,
    first_moment,
    second_moment,
):
    vmem = pl.BlockSpec(memory_space=pltpu.VMEM)
    hbm = pl.BlockSpec(memory_space=pl.ANY)
    dma = pltpu.SemaphoreType.DMA
    bf, f32, i32 = jnp.bfloat16, jnp.float32, jnp.int32

    def buf(*shape, kind=bf):
        return pltpu.VMEM(shape, kind)

    outs = pl.pallas_call(
        kernel,
        out_shape=(
            jax.ShapeDtypeStruct((128, 5120), bf),
            jax.ShapeDtypeStruct((160, 512), bf),
            jax.ShapeDtypeStruct((10, 512), bf),
            jax.ShapeDtypeStruct((10, 512), bf),
        ),
        in_specs=[hbm] * 10 + [vmem] * 2,
        out_specs=(hbm, vmem, vmem, vmem),
        scratch_shapes=[
            buf(128, 2560),
            buf(128, 2560),
            buf(128, 512),
            buf(128, 5120),
            buf(160, 512),
            buf(1, 128, kind=f32),
            buf(1, 128, kind=f32),
            buf(1, 32, kind=f32),
            buf(1, 32, kind=i32),
            buf(1, 32, kind=i32),
            buf(NZ, 4, 32, 512),
            buf(128, 2560),
            buf(64, 2560),
            buf(64, 2560),
            buf(KVH, QB, HEAD),
            buf(KVH, QB, HEAD),
            buf(8, KVH, 256, QB),
            buf(8, KVH, 1, QB, kind=f32),
            buf(KVH, 1, QB, kind=f32),
            buf(KVH, 1, QB, kind=f32),
            buf(2, 256, 512, kind=f32),
            buf(128, 512, kind=f32),
            buf(2, 8, 4, 32, 512),
            buf(2, 8, 4, 32, 512),
            buf(64, 512),
            buf(128, 5120),
            buf(8, 4, 160, 128),
            buf(4, 160, 1024),
            buf(32, 160, 512),
            buf(32, 512),
            buf(16, 32, 512),
            buf(160, 512, kind=f32),
            buf(160, 512, kind=f32),
            buf(8, 128, 512),
            buf(640, 512, kind=f32),
            buf(3, 640, 128),
            buf(3, 640, 128),
            buf(4, 160, 128, kind=f32),
            buf(4, 160, 128),
            buf(NZ, 160, 128),
            buf(160, 128),
            buf(4, 160, 128),
            dma((10,)),
            dma((6,)),
            dma((6,)),
            dma((2, 8, 4)),
            dma((2, 8, 4)),
            dma((2, 8, 4)),
            dma((2, 8, 4)),
            dma((8,)),
            dma((8,)),
            dma((2, 8)),
            dma((2, 8)),
            dma((4,)),
            dma((4,)),
            dma((16,)),
            dma((16,)),
            dma((8, 2)),
            dma((8, 2)),
            dma((3, 2)),
            dma((3, 2)),
            dma((4,)),
            dma((16,)),
            dma((3,)),
            dma,
            dma((4,)),
            dma((4,)),
            pltpu.SemaphoreType.REGULAR((4,)),
        ],
        compiler_params=pltpu.CompilerParams(
            collective_id=0, has_side_effects=True, vmem_limit_bytes=60 * 1024 * 1024
        ),
    )(
        attn_inputs,
        queries,
        key_vectors,
        logp_grad,
        new_logp.reshape(1, 128),
        old_logp.reshape(1, 128),
        rewards.reshape(1, 32),
        group_ids.reshape(1, 32),
        lengths.reshape(1, 32),
        value_proj,
        first_moment,
        second_moment,
    )
    return pl.pallas_call(
        hand_over,
        out_shape=[jax.ShapeDtypeStruct(o.shape, o.dtype) for o in outs],
        in_specs=[hbm, hbm, vmem, vmem],
        out_specs=[hbm, hbm, vmem, vmem],
        scratch_shapes=[buf(128, 5120), buf(160, 512), dma((5,)), dma((5,))],
        compiler_params=pltpu.CompilerParams(vmem_limit_bytes=60 * 1024 * 1024),
    )(*outs)


def hand_over(
    ig_in, np_in, nf_in, ns_in, ig_out, np_out, nf_out, ns_out, ig_mid, np_mid, sem_in, sem_out
):
    def pieces(ig_from, np_from, ig_to, np_to, sem):
        copies = [pltpu.make_async_copy(np_from, np_to, sem.at[0])]
        for i in range(4):
            rows = pl.ds(32 * i, 32)
            copies.append(
                pltpu.make_async_copy(ig_from.at[rows], ig_to.at[rows], sem.at[i + 1])
            )
        return copies

    fetched = pieces(ig_in, np_in, ig_mid, np_mid, sem_in)
    stored = pieces(ig_mid, np_mid, ig_out, np_out, sem_out)
    for copy in fetched:
        copy.start()
    nf_out[...] = nf_in[...]
    ns_out[...] = ns_in[...]
    for before, after in zip(fetched, stored):
        before.wait()
        after.start()
    for copy in stored:
        copy.wait()


def solution(mesh):
    torus = Mesh(mesh.devices.reshape(2, 16, 4, 2, 2), AXES)
    placed = (
        P(SIDE_FSDP, None),
        P(SIDE_FSDP, None),
        P(SIDE_FSDP, None),
        P(SIDE_FSDP, None),
        P(SIDE_FSDP),
        P(SIDE_FSDP),
        P(),
        P(),
        P(),
        P(FSDP, None),
        P(FSDP_SIDE, None),
        P(FSDP_SIDE, None),
    )
    return jax.shard_map(
        shards,
        mesh=torus,
        in_specs=placed,
        out_specs=(P(SIDE_FSDP, None), P(FSDP, None), P(FSDP_SIDE, None), P(FSDP_SIDE, None)),
        check_vma=False,
    )
```

```python
import math

import jax
import jax.numpy as jnp
from jax import lax
from jax.experimental import pallas as pl
from jax.experimental.pallas import tpu as pltpu
from jax.sharding import Mesh
from jax.sharding import PartitionSpec as P

AXES = ("xl", "z", "y", "xh", "core")
FSDP = ("xl", "z")
SIDE = ("y", "xh", "core")
SIDE_FSDP = SIDE + FSDP
FSDP_SIDE = FSDP + SIDE
MESH = pl.DeviceIdType.MESH
NZ = 16
KVH = 4
PER = 5
HEAD = 128
QB = PER * 128
EXP_SCALE = math.log2(math.e) / math.sqrt(HEAD)
LOW = -1e30

clip_low = 0.8
clip_high = 1.2
decay_first = 0.9
decay_second = 0.95
step_rate = 0.001
weight_decay = 0.1
adam_eps = 1e-08
bias_first = 1.0 - 0.9**10
bias_second = 1.0 - 0.95**10


def coefficient_row(new_ref, old_ref, rew_ref, gid_ref, len_ref, side, first_pos):
    rew = rew_ref[...]
    gid = gid_ref[...]
    lens = len_ref[...]
    roll_of = lax.broadcasted_iota(jnp.int32, rew.shape, 1)
    adv_parts, len_parts = [], []
    for roll in range(2):
        own = roll_of == side * 2 + roll
        own_gid = jnp.sum(jnp.where(own, gid, 0), axis=1, keepdims=True)
        own_rew = jnp.sum(jnp.where(own, rew, 0.0), axis=1, keepdims=True)
        own_len = jnp.sum(jnp.where(own, lens, 0), axis=1, keepdims=True)
        member = jnp.where(gid == own_gid, 1.0, 0.0)
        count = jnp.maximum(jnp.sum(member, axis=1, keepdims=True), 1.0)
        mean = jnp.sum(member * rew, axis=1, keepdims=True) / count
        spread = rew - mean
        var = jnp.sum(member * (spread * spread), axis=1, keepdims=True) / count
        adv_parts.append((own_rew - mean) / jnp.maximum(jnp.sqrt(var), 1.0))
        len_parts.append(own_len)
    slot = lax.broadcasted_iota(jnp.int32, (1, 128), 1)
    first = slot < 64
    adv = jnp.where(first, adv_parts[0], adv_parts[1])
    length = jnp.where(first, len_parts[0], len_parts[1])
    pos = first_pos + jnp.where(first, slot, slot - 64)
    ratio = jnp.exp(new_ref[...] - old_ref[...])
    clipped = jnp.minimum(jnp.maximum(ratio, clip_low), clip_high)
    active = (ratio * adv <= clipped * adv) & (pos < length)
    return jnp.where(active, -adv * ratio * (2048.0 / length.astype(jnp.float32)), 0.0)


def adam_rows(weight_now, grad_rows, first_moment, second_moment):
    first = decay_first * first_moment + (1.0 - decay_first) * grad_rows
    second = decay_second * second_moment + (1.0 - decay_second) * grad_rows * grad_rows
    update = (
        first / bias_first / (jnp.sqrt(second / bias_second) + adam_eps) + weight_decay * weight_now
    )
    return weight_now - step_rate * update, first, second


def kernel(
    x_hbm,
    q_hbm,
    k_hbm,
    g_hbm,
    new_hbm,
    old_hbm,
    rew_hbm,
    gid_hbm,
    len_hbm,
    w_hbm,
    m1_ref,
    m2_ref,
    ig_ref,
    np_ref,
    nf_ref,
    ns_ref,
    qv,
    gv,
    kv,
    xv,
    wv,
    newv,
    oldv,
    rewv,
    gidv,
    lenv,
    kbuf,
    gsend,
    qst,
    gst,
    qh,
    gh,
    eb,
    mst,
    mrow,
    lrow,
    pbuf,
    pown,
    rsend,
    rrecv,
    vsend,
    igv,
    xt,
    xg,
    wfull,
    mv,
    moms,
    m1f,
    m2f,
    vga,
    acc,
    xs,
    xr,
    zsum,
    zs,
    zr,
    gy,
    gf,
    load_sem,
    x_send,
    x_recv,
    ag_send,
    ag_recv,
    rs_send,
    rs_recv,
    in_send,
    in_recv,
    wz_send,
    wz_recv,
    wy_send,
    wy_recv,
    mo_send,
    mo_recv,
    va_send,
    va_recv,
    xs_send,
    xs_recv,
    zs_send,
    zs_recv,
    gy_send,
    gy_recv,
    gf_send,
    gf_recv,
    known,
):
    xl = lax.axis_index("xl")
    z = lax.axis_index("z")
    y = lax.axis_index("y")
    xh = lax.axis_index("xh")
    core = lax.axis_index("core")
    side = (y * 2 + xh) * 2 + core
    x = xh * 2 + xl
    up = lax.rem(z + 1, NZ)
    down = lax.rem(z + NZ - 1, NZ)
    mine = pl.ds(pl.multiple_of(64 * xl, 64), 64)
    theirs = pl.ds(pl.multiple_of(64 * (1 - xl), 64), 64)

    def lanes(index):
        return pl.ds(pl.multiple_of(index * 128, 128), 128)

    def y_at(step):
        return lax.rem(y + step, 4)

    loads = [
        pltpu.make_async_copy(src, dst, load_sem.at[i])
        for i, (src, dst) in enumerate(
            (
                (k_hbm, kv),
                (q_hbm, qv),
                (w_hbm, wv),
                (new_hbm, newv),
                (old_hbm, oldv),
                (rew_hbm, rewv),
                (gid_hbm, gidv),
                (len_hbm, lenv),
                (g_hbm, gv),
                (x_hbm, xv),
            )
        )
    ]
    loads[0].start()
    barrier = pltpu.get_barrier_semaphore()

    def greet(**where):
        pl.semaphore_signal(barrier, inc=1, device_id=where, device_id_type=MESH)

    beside = [{"xl": 1 - xl, "xh": xh}, {"xl": 1 - xl, "xh": 1 - xh}]
    around = [{"y": y_at(1)}, {"y": y_at(3)}]
    greet(z=up)
    greet(z=down)
    greet(**beside[0])
    greet(core=1 - core)
    for where in around + beside[1:]:
        greet(**where)

    def hello(kind, to):
        for where in to:
            pl.semaphore_signal(known.at[kind], inc=1, device_id=where, device_id_type=MESH)

    def heard(kind, to):
        pl.semaphore_wait(known.at[kind], len(to))

    for load in loads[1:]:
        load.start()
    loads[0].wait()
    kbuf[z, pl.ds(2 * xl, 2)] = kv[mine, :].reshape(2, 32, 512)
    pl.semaphore_wait(barrier, 7)

    def copy_to(src, dst, send, recv, **where):
        return pltpu.make_async_remote_copy(
            src_ref=src,
            dst_ref=dst,
            send_sem=send,
            recv_sem=recv,
            device_id=where,
            device_id_type=MESH,
        )

    def pair_copy(src, dst, at):
        return copy_to(src, dst, x_send.at[at], x_recv.at[at], xl=1 - xl)

    def ring_block(way, step):
        back = step - 1
        return lax.rem(z + NZ - back, NZ) if way == 0 else lax.rem(z + back, NZ)

    def key_copy(way, step, piece):
        part = kbuf.at[ring_block(way, step), piece]
        return copy_to(
            part,
            part,
            ag_send.at[way, step - 1, piece],
            ag_recv.at[way, step - 1, piece],
            z=up if way == 0 else down,
        )

    def weight_copy(way, step):
        part = wfull.at[core * NZ + ring_block(way, step), :, lanes(y)]
        return copy_to(
            part,
            part,
            wz_send.at[way, step - 1],
            wz_recv.at[way, step - 1],
            z=up if way == 0 else down,
        )

    def part_copy(way, step, piece):
        return copy_to(
            rsend.at[way, step, piece],
            rrecv.at[way, step, piece],
            rs_send.at[way, step, piece],
            rs_recv.at[way, step, piece],
            z=up if way == 0 else down,
        )

    def key_pair(i):
        rows = pl.ds(pl.multiple_of(64 * (1 - xl) + 32 * i, 32), 32)
        return pair_copy(kv.at[rows], kbuf.at[z, 2 * xl + i], 5 * i)

    query_pair = pair_copy(qv.at[theirs], qst, 1)
    grad_pair = pair_copy(gsend.at[theirs], gst, 2)
    own_weight = wfull.at[core * NZ + z, :, lanes(y)]
    weight_pair = pair_copy(wv.at[:, lanes(y)], own_weight, 3)
    for i in range(2):
        key_pair(i).start()
        for way in range(2):
            key_copy(way, 1, 2 * xl + i).start()
    for i in range(1, 3):
        loads[i].wait()

    @pl.when(core == xl)
    def _():
        weight_pair.start()
        wfull[core * NZ + z, :, lanes(y)] = wv[:, lanes(y)]

    query_pair.start()
    hello(0, around + beside[:1] + [{"core": 1 - core}])

    for i in range(3, 9):
        loads[i].wait()
    coeff = coefficient_row(newv, oldv, rewv, gidv, lenv, side, (xl * NZ + z) * 64)
    diag = lax.broadcasted_iota(jnp.int32, (128, 128), 0) == lax.broadcasted_iota(
        jnp.int32, (128, 128), 1
    )
    coeff_col = jnp.sum(jnp.where(diag, coeff, 0.0), axis=1, keepdims=True)
    for head in range(KVH * PER):
        cols = slice(head * HEAD, (head + 1) * HEAD)
        gsend[:, cols] = (coeff_col * gv[:, cols].astype(jnp.float32)).astype(jnp.bfloat16)
    grad_pair.start()
    for i in range(2):
        key_pair(i).wait_recv()
        for way in range(2):
            key_copy(way, 1, 2 * (1 - xl) + i).start()


    @pl.when(core != xl)
    def _():
        weight_pair.wait_recv()

    for way in range(2):
        weight_copy(way, 1).start()

    def spread(dst, src, rows, half, group):
        for head in range(PER):
            at = pl.ds(pl.multiple_of(64 * half, 64) + head * 128, 64)
            col = (group * PER + head) * HEAD
            dst[group, at, :] = src[rows, col : col + HEAD]

    mrow[...] = jnp.full(mrow.shape, LOW, jnp.float32)
    lrow[...] = jnp.zeros(lrow.shape, jnp.float32)

    def arrived(step, work):
        last = isinstance(step, int) and step == 8
        for i in range(4):
            piece = lax.rem(2 * xl + i, 4)
            key_copy(0, step, piece).wait_recv()
            if last:
                work(i)
                continue
            key_copy(0, step + 1, piece).start()
            key_copy(1, step, piece).wait_recv()

            @pl.when(step < 7)
            def _():
                key_copy(1, step + 1, piece).start()

            work(i)
        weight_copy(0, step).wait_recv()
        if last:
            return
        weight_copy(0, step + 1).start()
        weight_copy(1, step).wait_recv()

        @pl.when(step < 7)
        def _():
            weight_copy(1, step + 1).start()

    loads[9].wait()

    def turn(n):
        xt[n] = xv[:, n * 640 : (n + 1) * 640].T.reshape(4, 160, 128)

    def input_copies():
        copies = []
        for step in range(4):
            for flip in range(2):
                if step + flip:
                    there = core ^ flip
                    copies.append(
                        copy_to(
                            xt.at[pl.ds(4 * there, 4), y_at(step)],
                            xg.at[:, :, lanes(2 * y + core)],
                            in_send.at[step * 2 + flip],
                            in_recv.at[step * 2 + flip],
                            y=y_at(step),
                            core=there,
                        )
                    )
        return copies

    def moment_copies():
        copies = []
        for step in range(4):
            for flip in range(4):
                if step + flip:
                    copies.append(
                        copy_to(
                            mv,
                            moms.at[side],
                            mo_send.at[step * 4 + flip],
                            mo_recv.at[step * 4 + flip],
                            y=y_at(step),
                            xh=xh ^ (flip & 1),
                            core=core ^ (flip >> 1),
                        )
                    )
        return copies

    mv[...] = jnp.zeros(mv.shape, mv.dtype)
    mv[0:10, :] = m1_ref[...]
    mv[16:26, :] = m2_ref[...]
    moms[side] = mv[...]

    row = lax.broadcasted_iota(jnp.int32, (256, 1), 0)
    lane = lax.broadcasted_iota(jnp.int32, (1, QB), 1)
    in_head = lax.rem(lane, 128)
    qpos = jnp.where(in_head < 64, in_head, in_head - 64 + 1024) + z * 64
    in_block = lax.rem(row, 128)
    kpos_base = jnp.where(in_block < 64, in_block, in_block - 64 + 1024)

    def score(index):
        t = index // KVH + 1
        head = lax.rem(index, KVH)
        a = lax.rem(z + NZ - t, NZ)
        b = lax.rem(z + jnp.where(t == 8, 0, t), NZ)
        keys = jnp.concatenate(
            [
                kbuf[a, :, :, lanes(head)].reshape(128, HEAD),
                kbuf[b, :, :, lanes(head)].reshape(128, HEAD),
            ],
            axis=0,
        )
        s = lax.dot_general(
            keys, qh[head], (((1,), (1,)), ((), ())), preferred_element_type=jnp.float32
        )
        kpos = kpos_base + jnp.where(row < 128, a, b) * 64
        s = jnp.where(kpos <= qpos, s, LOW)
        old = mrow[head]
        top = jnp.maximum(old, jnp.max(s, axis=0, keepdims=True))
        e = jnp.exp2((s - top) * EXP_SCALE)
        lrow[head] = lrow[head] * jnp.exp2((old - top) * EXP_SCALE) + jnp.sum(
            e, axis=0, keepdims=True
        )
        mrow[head] = top
        mst[t - 1, head] = top
        eb[t - 1, head] = e.astype(jnp.bfloat16)

    arrived(1, lambda i: spread(qh, qv, mine, xl, i))
    heard(0, range(4))
    hello(1, [{"core": 1 - core}])
    arrived(2, lambda i: turn(i))
    heard(1, range(1))
    hello(2, beside)
    arrived(3, lambda i: turn(4 + i))
    heard(2, range(2))
    hello(3, beside)
    for copy in input_copies():
        copy.start()
    query_pair.wait_recv()

    def second_half(i):
        spread(qh, qst, slice(None), 1 - xl, i)
        spread(gh, gsend, mine, xl, i)

    arrived(4, second_half)
    heard(3, range(2))
    for copy in moment_copies():
        copy.start()

    def key_step(step, carry):
        def work(i):
            for unit in range(2):
                score((step - 5) * 8 + i * 2 + unit)

        arrived(step, work)
        return carry

    lax.fori_loop(5, 8, key_step, 0)
    xg[:, :, lanes(2 * y + core)] = xt[pl.ds(4 * core, 4), y]
    grad_pair.wait_recv()

    def last_step(i):
        score(24 + i)
        spread(gh, gst, slice(None), 1 - xl, i)

    arrived(8, last_step)

    def across_y(step):
        part = wfull.at[pl.ds(NZ * core, NZ), :, lanes(y)]
        return copy_to(part, part, wy_send.at[step], wy_recv.at[step], y=y_at(step))

    def across_core():
        part = wfull.at[pl.ds(NZ * core, NZ)]
        return copy_to(part, part, wy_send.at[0], wy_recv.at[0], core=1 - core)

    for step in range(1, 4):
        across_y(step).start()
    for head in range(KVH):
        score(28 + head)

    lrow[...] = 1.0 / lrow[...]

    def parts(t, dst, head):
        scale = jnp.exp2((mst[t - 1, head] - mrow[head]) * EXP_SCALE) * lrow[head]
        p = (eb[t - 1, head].astype(jnp.float32) * scale).astype(jnp.bfloat16)
        dst[:, head * HEAD : (head + 1) * HEAD] = jnp.dot(
            p, gh[head], preferred_element_type=jnp.float32
        )

    def pass_on(way, step, src, piece, first):
        piece = lax.rem(piece + 2 * (1 - xl), 4)
        value = src[pl.ds(pl.multiple_of(piece * 32, 32), 32), :]
        if not first:
            part_copy(way, step - 1, piece).wait_recv()
            value = value + rrecv[way, step - 1, piece].astype(jnp.float32)
        rsend[way, step, piece] = value.astype(jnp.bfloat16)
        part_copy(way, step, piece).start()

    for head in range(KVH):
        parts(8, pbuf.at[0], head)
    for piece in range(4):
        pass_on(0, 0, pbuf.at[0, pl.ds(0, 128)], piece, True)
    pown[...] = pbuf[0, 128:256, :]
    for head in range(KVH):
        parts(7, pbuf.at[1], head)
    for piece in range(4):
        pass_on(1, 0, pbuf.at[1, pl.ds(0, 128)], piece, True)
    for head in range(KVH):
        parts(6, pbuf.at[0], head)
    for piece in range(4):
        pass_on(0, 1, pbuf.at[1, pl.ds(128, 128)], piece, False)

    def ring_step(i, carry):
        now = pbuf.at[lax.rem(i, 2)]
        later = pbuf.at[1 - lax.rem(i, 2)]
        for piece in range(4):
            pass_on(1, i - 1, now.at[pl.ds(0, 128)], piece, False)
            pass_on(0, i, now.at[pl.ds(128, 128)], piece, False)
            parts(7 - i, later, piece)
        return carry

    lax.fori_loop(2, 7, ring_step, 0)
    for piece in range(4):
        pass_on(1, 6, pbuf.at[1, pl.ds(0, 128)], piece, False)
        pass_on(0, 7, pbuf.at[1, pl.ds(128, 128)], piece, False)

    slot = 2 * y + core
    value_pair = pair_copy(vsend, vga.at[slot, mine], 4)

    def block_rows(half):
        for i in range(2):
            part_copy(1, 6, 2 * half + i).wait_recv()
            part_copy(0, 7, 2 * half + i).wait_recv()
        rows = pl.ds(2 * half, 2)
        return (
            pown[pl.ds(pl.multiple_of(64 * half, 64), 64), :]
            + rrecv[1, 6, rows].reshape(64, 512).astype(jnp.float32)
            + rrecv[0, 7, rows].reshape(64, 512).astype(jnp.float32)
        ).astype(jnp.bfloat16)

    def value_part(at, part):
        return vga.at[at, theirs if part else mine]

    def values_y(step, part):
        rows = value_part(slot, part)
        return copy_to(
            rows, rows, va_send.at[step, part], va_recv.at[step, part], y=y_at(step)
        )

    def values_core(step, part):
        rows = value_part(2 * lax.rem(y + 4 - step, 4) + core, part)
        return copy_to(
            rows, rows, va_send.at[4 + step, part], va_recv.at[4 + step, part], core=1 - core
        )

    vsend[...] = block_rows(1 - xl)
    value_pair.start()
    vga[slot, mine, :] = block_rows(xl)
    for step in (2, 1, 3):
        values_y(step, 0).start()
    values_core(0, 0).start()
    value_pair.wait_recv()
    for step in (2, 1, 3):
        values_y(step, 1).start()
    values_core(0, 1).start()

    for copy in input_copies():
        copy.wait_recv()

    def add_inputs(step, first):
        at = lax.rem(y + 4 - step, 4)
        a = xg[:, :, pl.ds(pl.multiple_of(at * 256, 256), 256)].reshape(640, 256)
        b = vga[pl.ds(2 * at, 2)].reshape(256, 512)
        value = jnp.dot(a, b, preferred_element_type=jnp.float32)
        acc[...] = value if first else acc[...] + value

    for step in (1, 3, 2):
        values_y(step, 0).wait_recv()
        values_core(step, 0).start()
    for part in range(2):
        values_core(0, part).wait_recv()
    add_inputs(0, True)
    for step in (1, 3, 2):
        values_y(step, 1).wait_recv()
        values_core(step, 1).start()
        for part in range(2):
            values_core(step, part).wait_recv()
        add_inputs(step, False)

    def sum_x(step, half):
        at = lax.rem(x + step, 4)
        rows = pl.ds(320 * half, 320)
        return copy_to(
            xs.at[step - 1, rows],
            xr.at[step - 1, rows],
            xs_send.at[step - 1, half],
            xs_recv.at[step - 1, half],
            xl=lax.rem(at, 2),
            xh=at // 2,
        )

    for half in range(2):
        rows = pl.ds(320 * half, 320)
        for step in (2, 1, 3):
            at = lax.rem(x + step, 4)
            xs[step - 1, rows] = acc[rows, lanes(at)].astype(jnp.bfloat16)
            sum_x(step, half).start()

    for step in range(1, 4):
        across_y(step).wait_recv()
    across_core().start()

    for copy in moment_copies():
        copy.wait_recv()
    for s in range(16):
        m1f[10 * s : 10 * s + 10, :] = moms[s, 0:10, :].astype(jnp.float32)
        m2f[10 * s : 10 * s + 10, :] = moms[s, 16:26, :].astype(jnp.float32)

    def grad_tile(n, carry):
        w = wfull[pl.ds(4 * n, 4)].reshape(640, 512)
        igv[:, pl.ds(pl.multiple_of(n * 640, 128), 640)] = lax.dot_general(
            vga[slot], w, (((1,), (1,)), ((), ())), preferred_element_type=jnp.float32
        ).astype(jnp.bfloat16)
        return carry

    lax.fori_loop(4 * core, 4 * core + 4, grad_tile, 0)

    for way in range(2):
        for step in range(8 - way):
            weight_copy(way, step + 1).wait_send()
            for piece in range(4):
                key_copy(way, step + 1, piece).wait_send()
    for copy in [key_pair(0), key_pair(1), query_pair, grad_pair] + input_copies():
        copy.wait_send()

    @pl.when(core == xl)
    def _():
        weight_pair.wait_send()

    def sum_z(j):
        at = 4 * j + y
        far = lax.rem(z - at + NZ, NZ)
        return copy_to(zs.at[j], zr.at[far], zs_send.at[j], zs_recv.at[far], z=at)

    for half in range(2):
        rows = pl.ds(320 * half, 320)
        total = acc[rows, lanes(x)]
        for step in (1, 3, 2):
            sum_x(step, half).wait_recv()
            total = total + xr[step - 1, rows].astype(jnp.float32)
        zsum[2 * half : 2 * half + 2] = total.reshape(2, 160, 128)
        zs[2 * half : 2 * half + 2] = total.reshape(2, 160, 128).astype(jnp.bfloat16)
        for j in range(2 * half, 2 * half + 2):

            @pl.when(z != 4 * j + y)
            def _(j=j):
                sum_z(j).start()

    across_core().wait_recv()
    lax.fori_loop(4 * (1 - core), 4 * (1 - core) + 4, grad_tile, 0)
    grad_out = [
        pltpu.make_async_copy(igv.at[pl.ds(32 * i, 32)], ig_ref.at[pl.ds(32 * i, 32)], load_sem.at[i])
        for i in range(4)
    ]
    for out in grad_out:
        out.start()
    root = lax.rem(z, 4) == y

    def spread_y(step):
        return copy_to(gy, gy, gy_send.at[step - 1], gy_recv, y=y_at(step))

    @pl.when(root)
    def _():
        total = zsum[z // 4]
        for far in range(1, NZ):
            copy_to(zs.at[0], zr.at[far], zs_send.at[0], zs_recv.at[far], z=up).wait_recv()
            total = total + zr[far].astype(jnp.float32)
        gy[...] = total.astype(jnp.bfloat16)
        for step in range(1, 4):
            spread_y(step).start()

    @pl.when(jnp.logical_not(root))
    def _():
        spread_y(1).wait_recv()

    def spread_x(to_xh, to_core):
        k = to_xh * 2 + to_core
        return copy_to(
            gy, gf.at[x], gf_send.at[k], gf_recv.at[x], xl=core, xh=to_xh, core=to_core
        )

    def is_self(to_xh, to_core):
        return (xl == core) & (xh == to_xh) & (core == to_core)

    for to_xh in range(2):
        for to_core in range(2):

            @pl.when(jnp.logical_not(is_self(to_xh, to_core)))
            def _(to_xh=to_xh, to_core=to_core):
                spread_x(to_xh, to_core).start()

    @pl.when(xl == core)
    def _():
        gf[x] = gy[...]

    for way in range(2):
        for step in range(8 - way):
            for piece in range(4):
                part_copy(way, step, piece).wait_send()
    value_pair.wait_send()
    for copy in moment_copies():
        copy.wait_send()
    for step in range(1, 4):
        across_y(step).wait_send()
        for half in range(2):
            values_y(step, half).wait_send()
            sum_x(step, half).wait_send()
    for step in range(4):
        for part in range(2):
            values_core(step, part).wait_send()

    for at in range(4):

        @pl.when(jnp.logical_not((xl == core) & (x == at)))
        def _(at=at):
            copy_to(gy, gf.at[at], gf_send.at[0], gf_recv.at[at], core=1 - core).wait_recv()

        cols = slice(at * 128, (at + 1) * 128)
        new, first, second = adam_rows(
            wv[:, cols].astype(jnp.float32),
            gf[at].astype(jnp.float32),
            m1f[:, cols],
            m2f[:, cols],
        )
        np_ref[:, cols] = new.astype(jnp.bfloat16)
        m1f[:, cols] = first
        m2f[:, cols] = second
    for s in range(16):

        @pl.when(side == s)
        def _(s=s):
            nf_ref[...] = m1f[10 * s : 10 * s + 10, :].astype(jnp.bfloat16)
            ns_ref[...] = m2f[10 * s : 10 * s + 10, :].astype(jnp.bfloat16)

    across_core().wait_send()
    for out in grad_out:
        out.wait()
    for j in range(4):

        @pl.when(z != 4 * j + y)
        def _(j=j):
            sum_z(j).wait_send()

    @pl.when(root)
    def _():
        for step in range(1, 4):
            spread_y(step).wait_send()

    for to_xh in range(2):
        for to_core in range(2):

            @pl.when(jnp.logical_not(is_self(to_xh, to_core)))
            def _(to_xh=to_xh, to_core=to_core):
                spread_x(to_xh, to_core).wait_send()


def shards(
    attn_inputs,
    queries,
    key_vectors,
    logp_grad,
    new_logp,
    old_logp,
    rewards,
    group_ids,
    lengths,
    value_proj,
    first_moment,
    second_moment,
):
    vmem = pl.BlockSpec(memory_space=pltpu.VMEM)
    hbm = pl.BlockSpec(memory_space=pl.ANY)
    dma = pltpu.SemaphoreType.DMA
    bf, f32, i32 = jnp.bfloat16, jnp.float32, jnp.int32

    def buf(*shape, kind=bf):
        return pltpu.VMEM(shape, kind)

    outs = pl.pallas_call(
        kernel,
        out_shape=(
            jax.ShapeDtypeStruct((128, 5120), bf),
            jax.ShapeDtypeStruct((160, 512), bf),
            jax.ShapeDtypeStruct((10, 512), bf),
            jax.ShapeDtypeStruct((10, 512), bf),
        ),
        in_specs=[hbm] * 10 + [vmem] * 2,
        out_specs=(hbm, vmem, vmem, vmem),
        scratch_shapes=[
            buf(128, 2560),
            buf(128, 2560),
            buf(128, 512),
            buf(128, 5120),
            buf(160, 512),
            buf(1, 128, kind=f32),
            buf(1, 128, kind=f32),
            buf(1, 32, kind=f32),
            buf(1, 32, kind=i32),
            buf(1, 32, kind=i32),
            buf(NZ, 4, 32, 512),
            buf(128, 2560),
            buf(64, 2560),
            buf(64, 2560),
            buf(KVH, QB, HEAD),
            buf(KVH, QB, HEAD),
            buf(8, KVH, 256, QB),
            buf(8, KVH, 1, QB, kind=f32),
            buf(KVH, 1, QB, kind=f32),
            buf(KVH, 1, QB, kind=f32),
            buf(2, 256, 512, kind=f32),
            buf(128, 512, kind=f32),
            buf(2, 8, 4, 32, 512),
            buf(2, 8, 4, 32, 512),
            buf(64, 512),
            buf(128, 5120),
            buf(8, 4, 160, 128),
            buf(4, 160, 1024),
            buf(32, 160, 512),
            buf(32, 512),
            buf(16, 32, 512),
            buf(160, 512, kind=f32),
            buf(160, 512, kind=f32),
            buf(8, 128, 512),
            buf(640, 512, kind=f32),
            buf(3, 640, 128),
            buf(3, 640, 128),
            buf(4, 160, 128, kind=f32),
            buf(4, 160, 128),
            buf(NZ, 160, 128),
            buf(160, 128),
            buf(4, 160, 128),
            dma((10,)),
            dma((6,)),
            dma((6,)),
            dma((2, 8, 4)),
            dma((2, 8, 4)),
            dma((2, 8, 4)),
            dma((2, 8, 4)),
            dma((8,)),
            dma((8,)),
            dma((2, 8)),
            dma((2, 8)),
            dma((4,)),
            dma((4,)),
            dma((16,)),
            dma((16,)),
            dma((8, 2)),
            dma((8, 2)),
            dma((3, 2)),
            dma((3, 2)),
            dma((4,)),
            dma((16,)),
            dma((3,)),
            dma,
            dma((4,)),
            dma((4,)),
            pltpu.SemaphoreType.REGULAR((4,)),
        ],
        compiler_params=pltpu.CompilerParams(
            collective_id=0, has_side_effects=True, vmem_limit_bytes=60 * 1024 * 1024
        ),
    )(
        attn_inputs,
        queries,
        key_vectors,
        logp_grad,
        new_logp.reshape(1, 128),
        old_logp.reshape(1, 128),
        rewards.reshape(1, 32),
        group_ids.reshape(1, 32),
        lengths.reshape(1, 32),
        value_proj,
        first_moment,
        second_moment,
    )
    return pl.pallas_call(
        hand_over,
        out_shape=[jax.ShapeDtypeStruct(o.shape, o.dtype) for o in outs],
        in_specs=[vmem] * 4,
        out_specs=[vmem] * 4,
        compiler_params=pltpu.CompilerParams(vmem_limit_bytes=60 * 1024 * 1024),
    )(*outs)


def hand_over(ig_in, np_in, nf_in, ns_in, ig_out, np_out, nf_out, ns_out):
    ig_out[...] = ig_in[...]
    np_out[...] = np_in[...]
    nf_out[...] = nf_in[...]
    ns_out[...] = ns_in[...]


def solution(mesh):
    torus = Mesh(mesh.devices.reshape(2, 16, 4, 2, 2), AXES)
    placed = (
        P(SIDE_FSDP, None),
        P(SIDE_FSDP, None),
        P(SIDE_FSDP, None),
        P(SIDE_FSDP, None),
        P(SIDE_FSDP),
        P(SIDE_FSDP),
        P(),
        P(),
        P(),
        P(FSDP, None),
        P(FSDP_SIDE, None),
        P(FSDP_SIDE, None),
    )
    return jax.shard_map(
        shards,
        mesh=torus,
        in_specs=placed,
        out_specs=(P(SIDE_FSDP, None), P(FSDP, None), P(FSDP_SIDE, None), P(FSDP_SIDE, None)),
        check_vma=False,
    )
```
